32 devices in a mesh: seq: 8 (over y, x, core), tensor: 4 (over z).
Axes of the slice: x: 2, y: 2, z: 4, core: 2. Of those that a mesh axis runs over, the one named last changes fastest.
Arguments:
- ssd_input: bfloat16 [3072, 8192], P('seq', 'tensor'), may hold values from -6 to 6
- gate_input: bfloat16 [3072, 8192], P('seq', 'tensor'), may hold values from -6 to 6
- state_maps: bfloat16 [3072, 2, 2048], P('seq', None, 'tensor'), may hold values from -2 to 2
- step_raw: float32 [3072, 64], P('seq', 'tensor'), may hold values from -3 to 3
- step_bias: float32 [64], P('tensor'), may hold values from -1 to 0
- decay_rate: float32 [64], P('tensor'), may hold values from 0.00043402778 to 0.1, as said below
- skip_gain: float32 [64], P('tensor'), may hold values from 0.5 to 1.5
- norm_gain: float32 [8192], P('tensor'), may hold values from 0.1 to 1.9
- out_weight: bfloat16 [4096, 8192], P(None, 'tensor'), may hold values from -0.176776695 to 0.176776695
- reward_head: float32 [4096], replicated, may hold values from -0.25 to 0.25
- traj_lengths: int32 [16], replicated, may hold values from 1 to 1152, 3072 in all
- step_pairs: int32 [3072], replicated, may hold values from 0 to 3071, each once
Outputs:
- rewards: float32 [3072], P('seq')
- grad_input: bfloat16 [3072, 8192], P('seq', 'tensor')
- grad_gate: bfloat16 [3072, 8192], P('seq', 'tensor')
- grad_maps: bfloat16 [3072, 2, 2048], P('seq', None, 'tensor')
- grad_step: float32 [3072, 64], P('seq', 'tensor')
The draws below stay inside these ranges and needn't reach their ends.
Inputs may be any that keep to these rules, and one draw needn't show every extreme that they name: `traj_lengths`: trajectory lengths sum to 3072; the longest is exactly 1152. A permutation of the token positions; step_pairs[2k] is the chosen and step_pairs[2k+1] the rejected step of pair k. `decay_rate`: positive decay rates.
All inputs are finite; a program needn't handle non-finite values.
Results may differ from the reference program's by a relative error of at most 0.006.
Values may be sent and summed in bfloat16 or wider, within the bound.
No kernel may reach another device: no remote copies, remote signals or barrier semaphores. Data moves between devices by JAX's collectives and lax.ppermute only.
A program may use at most 128 MiB of HBM per device.

```python
import math
import jax
import jax.numpy as jnp
import numpy as np
from jax import lax

D = 4096
HEADS = 64
HEAD_DIM = 128
STATE = 128
GROUPS = 16
TOK_DEV = 384
TOKENS = 3072
MAXTRAJ = 1152
NTRAJ = 16
N_SEQ = 8
N_TENSOR = 4


def rising(count, factor):
    return jnp.power(factor, jnp.arange(count, dtype=jnp.float32) / (count - 1))


def draw_decay_rate(key, part):
    low_end = math.log(1.0 / (2.0 * TOK_DEV))
    high_end = math.log(0.1)
    uniform_part = jax.random.uniform(key, (HEADS,), jnp.float32)
    return jnp.exp(low_end + (high_end - low_end) * uniform_part)


def draw_out_weight(key, part):
    fan_in = HEADS * HEAD_DIM
    base_draw = jnp.clip(jax.random.normal(key, (D, fan_in), jnp.float32), -4.0, 4.0)
    row_lift = rising(D, 3.0)
    return (base_draw * row_lift[:, None] * fan_in ** (-0.5)).astype(jnp.bfloat16)


def draw_reward_head(key, part):
    base_draw = jnp.clip(jax.random.normal(key, (D,), jnp.float32), -4.0, 4.0)
    row_lift = rising(D, 3.0)
    return base_draw * row_lift * D ** (-0.5)


def steps_of(stream_key, dims, pieces, low, top_value):
    loudness = 1.0
    for axis_at, parts in pieces:
        steps = jax.random.uniform(jax.random.fold_in(jax.random.fold_in(stream_key, 6), axis_at), (parts,), jnp.float32, low / len(pieces), top_value / len(pieces))
        loudness = loudness * jnp.repeat(jnp.exp(steps), dims[axis_at] // parts).reshape((-1,) + (1,) * (len(dims) - 1 - axis_at))
    return loudness


def split_up(number_of, total, reach, slope):
    weights = [(1 << 20) // math.isqrt(standing ** slope) + 1 for standing in range(2, number_of + 1)]
    rest, holding = total - reach - (number_of - 1), [1] * (number_of - 1)
    while rest > 0:
        movable = [i for i in range(number_of - 1) if holding[i] < reach]
        whole, remaining = sum([weights[i] for i in movable]), rest
        for i in movable:
            addition = min(reach - holding[i], max(1, remaining * weights[i] // whole), rest)
            holding[i] = holding[i] + addition
            rest = rest - addition
    return np.array([reach] + holding)


def uneven_parts(key, amount, total, reach, skew):
    if amount == 2:
        one = jax.random.randint(key, (), max(1, total - reach), min(reach, total - 1) + 1)
        return jnp.stack([one, total - one])
    tallies = jnp.asarray(split_up(amount, total, reach, skew), jnp.int32)
    couples = (amount - 1) // 2
    donor, sink = tallies[1:1 + 2 * couples:2], tallies[2:2 + 2 * couples:2]
    margin = jnp.minimum(donor - 1, reach - sink)
    shifted = jax.random.randint(jax.random.fold_in(key, 1), (couples,), 0, 1 << 20) % (margin + 1)
    tallies = tallies.at[1:1 + 2 * couples:2].set(donor - shifted).at[2:2 + 2 * couples:2].set(sink + shifted)
    return tallies[jax.random.permutation(jax.random.fold_in(key, 2), amount)]


def bell_draw(key, shape, deviation, bound, shards=(), kind=jnp.bfloat16):
    loudness = steps_of(key, shape, shards, -0.22, 0.18) if shards else 1.0
    values = jax.random.normal(key, shape, jnp.float32) * deviation * loudness
    return jnp.minimum(jnp.maximum(values, -bound), bound).astype(kind)


def setup_inputs(seed: int = 0) -> dict:
    splits = jax.random.split(jax.random.key(seed), 13)
    return {
        "ssd_input": bell_draw(splits[0], (TOKENS, HEADS * HEAD_DIM), 1.0, 6.0, ((0, 8), (1, 4))),
        "gate_input": bell_draw(splits[1], (TOKENS, HEADS * HEAD_DIM), 1.0, 6.0, ((0, 8), (1, 4))),
        "state_maps": bell_draw(splits[2], (TOKENS, 2, GROUPS * STATE), 0.3, 2.0, ((0, 8), (2, 4))),
        "step_raw": bell_draw(splits[3], (TOKENS, HEADS), 0.5, 3.0, ((0, 8), (1, 4)), jnp.float32),
        "step_bias": jnp.clip(-1.0 + 1.0 * jax.random.uniform(splits[4], (HEADS,), jnp.float32) ** steps_of(splits[4], (HEADS,), ((0, 4),), -0.2, 0.2), -1.0, 0.0),
        "decay_rate": draw_decay_rate(jax.random.fold_in(splits[12], 71), 0),
        "skip_gain": jnp.clip(0.5 + 1.0 * jax.random.uniform(splits[6], (HEADS,), jnp.float32) ** steps_of(splits[6], (HEADS,), ((0, 4),), -0.2, 0.2), 0.5, 1.5),
        "norm_gain": jnp.clip(1.0 + 0.18 * jax.random.normal(splits[7], (HEADS * HEAD_DIM,), jnp.float32), 0.1, 1.9),
        "out_weight": draw_out_weight(jax.random.fold_in(splits[12], 71), 0),
        "reward_head": draw_reward_head(jax.random.fold_in(splits[12], 71), 0),
        "traj_lengths": uneven_parts(splits[10], NTRAJ, TOKENS, MAXTRAJ, 2).astype(jnp.int32),
        "step_pairs": jax.random.permutation(splits[11], TOKENS).astype(jnp.int32),
    }


norm_eps = 1e-05
loss_scale = 64.0
highest = lax.Precision.HIGHEST

def prepare(step_raw, step_bias, decay_rate, starts):
    step_size = jax.nn.softplus(step_raw + step_bias[None, :])
    cumulative = jnp.cumsum(-step_size * decay_rate[None, :], axis=0)
    segment = jnp.cumsum(starts)
    return (step_size, cumulative, segment)

def local_out(x_heads, z_heads, b_rows, c_rows, step_raw, state_in, step_bias, decay_rate, skip_gain, norm_gain, starts):
    row_count, head_count, head_width = x_heads.shape
    group_count = b_rows.shape[1]
    per_group = head_count // group_count
    step_size, cumulative, segment = prepare(step_raw, step_bias, decay_rate, starts)
    earlier = jnp.arange(row_count)[None, :] <= jnp.arange(row_count)[:, None]
    same_segment = segment[:, None] == segment[None, :]
    allowed = (earlier & same_segment)[:, :, None]
    spread = cumulative[:, None, :] - cumulative[None, :, :]
    decay_matrix = jnp.where(allowed, jnp.exp(jnp.where(allowed, spread, 0.0)), 0.0)
    scores = jnp.einsum('tgn,sgn->tsg', c_rows, b_rows, precision=highest)
    mixing = decay_matrix.reshape(row_count, row_count, group_count, per_group) * scores[:, :, :, None] * step_size.reshape(1, row_count, group_count, per_group)
    grouped_x = x_heads.reshape(row_count, group_count, per_group, head_width)
    within_part = jnp.einsum('tsgh,sghp->tghp', mixing, grouped_x, precision=highest)
    carried = jnp.einsum('tgn,ghnp->tghp', c_rows, state_in.reshape(group_count, per_group, -1, head_width), precision=highest)
    first_weight = jnp.where(segment[:, None] == 0, jnp.exp(cumulative), 0.0)
    carried_part = carried * first_weight.reshape(row_count, group_count, per_group, 1)
    mixed_heads = within_part + carried_part + skip_gain.reshape(1, group_count, per_group, 1) * grouped_x
    gated_heads = mixed_heads * jax.nn.silu(z_heads.reshape(row_count, group_count, per_group, head_width))
    mean_square = lax.optimization_barrier(jnp.mean(gated_heads * gated_heads, axis=(2, 3), keepdims=True))
    normed = gated_heads * lax.rsqrt(mean_square + norm_eps) * norm_gain.reshape(1, group_count, per_group, head_width)
    return normed.reshape(row_count, head_count * head_width)

def local_state(x_heads, b_rows, step_raw, step_bias, decay_rate, starts):
    row_count, head_count, head_width = x_heads.shape
    group_count = b_rows.shape[1]
    per_group = head_count // group_count
    step_size, cumulative, segment = prepare(step_raw, step_bias, decay_rate, starts)
    last_segment = segment[-1]
    weight = jnp.where((segment == last_segment)[:, None], jnp.exp(cumulative[-1][None, :] - cumulative), 0.0) * step_size
    state_sum = jnp.einsum('sgn,sgh,sghp->ghnp', b_rows, weight.reshape(row_count, group_count, per_group), x_heads.reshape(row_count, group_count, per_group, head_width), precision=highest)
    through = jnp.where(last_segment == 0, jnp.exp(cumulative[-1]), 0.0)
    return (state_sum.reshape(head_count, -1, head_width), through)

def reference(ssd_input, gate_input, state_maps, step_raw, step_bias, decay_rate, skip_gain, norm_gain, out_weight, reward_head, traj_lengths, step_pairs):
    row_count = TOK_DEV
    head_count = HEADS // N_TENSOR
    group_count = GROUPS // N_TENSOR
    head_width = HEAD_DIM
    channel_count = head_count * head_width
    positions = jnp.arange(TOKENS, dtype=jnp.int32)
    openings = jnp.cumsum(traj_lengths) - traj_lengths
    starts = jnp.any(positions[:, None] == openings[None, :], axis=1).astype(jnp.float32)
    start_blocks = starts.reshape(N_SEQ, row_count)
    group_ids = jnp.arange(N_TENSOR, dtype=jnp.int32)

    def slices(group_index):
        x_blocks = lax.dynamic_slice_in_dim(ssd_input, group_index * channel_count, channel_count, 1).astype(jnp.float32).reshape(N_SEQ, row_count, head_count, head_width)
        z_blocks = lax.dynamic_slice_in_dim(gate_input, group_index * channel_count, channel_count, 1).astype(jnp.float32).reshape(N_SEQ, row_count, head_count, head_width)
        b_blocks = lax.dynamic_slice_in_dim(state_maps[:, 0], group_index * (group_count * STATE), group_count * STATE, 1).astype(jnp.float32).reshape(N_SEQ, row_count, group_count, STATE)
        c_blocks = lax.dynamic_slice_in_dim(state_maps[:, 1], group_index * (group_count * STATE), group_count * STATE, 1).astype(jnp.float32).reshape(N_SEQ, row_count, group_count, STATE)
        step_blocks = lax.dynamic_slice_in_dim(step_raw, group_index * head_count, head_count, 1).reshape(N_SEQ, row_count, head_count)
        bias_part = lax.dynamic_slice_in_dim(step_bias, group_index * head_count, head_count, 0)
        rate_part = lax.dynamic_slice_in_dim(decay_rate, group_index * head_count, head_count, 0)
        skip_part = lax.dynamic_slice_in_dim(skip_gain, group_index * head_count, head_count, 0)
        gain_part = lax.dynamic_slice_in_dim(norm_gain, group_index * channel_count, channel_count, 0)
        return (x_blocks, z_blocks, b_blocks, c_blocks, step_blocks, bias_part, rate_part, skip_part, gain_part)
    zero_state = jnp.zeros((head_count, STATE, head_width), jnp.float32)

    def forward_group(group_index):
        x_blocks, z_blocks, b_blocks, c_blocks, step_blocks, bias_part, rate_part, skip_part, gain_part = slices(group_index)

        def block_step(state_in, block_data):
            x_heads, z_heads, b_rows, c_rows, step_rows, start_rows = block_data
            normed = local_out(x_heads, z_heads, b_rows, c_rows, step_rows, state_in, bias_part, rate_part, skip_part, gain_part, start_rows)
            state_sum, through = local_state(x_heads, b_rows, step_rows, bias_part, rate_part, start_rows)
            return (through[:, None, None] * state_in + state_sum, normed.astype(jnp.bfloat16))
        _, mixed_blocks = lax.scan(block_step, zero_state, (x_blocks, z_blocks, b_blocks, c_blocks, step_blocks, start_blocks))
        return mixed_blocks.reshape(TOKENS, channel_count)
    mixed_groups = lax.map(forward_group, group_ids)
    mixed_all = jnp.moveaxis(mixed_groups, 0, 1).reshape(TOKENS, HEADS * HEAD_DIM)
    hidden = lax.dot_general(out_weight, mixed_all, (((1,), (1,)), ((), ())), preferred_element_type=jnp.float32)
    squares = lax.optimization_barrier(jnp.sum(hidden * hidden, axis=0))
    along = lax.optimization_barrier(jnp.sum(hidden * reward_head[:, None], axis=0))
    scale = jnp.sqrt(squares / D + norm_eps)
    rewards = along / scale
    chosen = step_pairs[0::2]
    rejected = step_pairs[1::2]
    pair_push = loss_scale * jax.nn.sigmoid(rewards[rejected] - rewards[chosen])
    pair_grad = jnp.zeros((TOKENS,), jnp.float32).at[chosen].add(-pair_push).at[rejected].add(pair_push)
    d_hidden = (pair_grad[None, :] * (reward_head[:, None] / scale[None, :] - along[None, :] * hidden / (D * scale * scale * scale)[None, :])).astype(jnp.bfloat16)
    d_mixed = lax.dot_general(d_hidden, out_weight, (((0,), (0,)), ((), ())), preferred_element_type=jnp.float32)

    def backward_group(group_index):
        x_blocks, z_blocks, b_blocks, c_blocks, step_blocks, bias_part, rate_part, skip_part, gain_part = slices(group_index)
        mixed_grads = lax.dynamic_slice_in_dim(d_mixed, group_index * channel_count, channel_count, 1).reshape(N_SEQ, row_count, channel_count)

        def first_pass(state_in, block_data):
            x_heads, z_heads, b_rows, c_rows, step_rows, start_rows, grad_rows = block_data

            def out_part(a_in, b_in, c_in, d_in, e_in, f_in):
                return local_out(a_in, b_in, c_in, d_in, e_in, f_in, bias_part, rate_part, skip_part, gain_part, start_rows)
            _, pull_back = jax.vjp(out_part, x_heads, z_heads, b_rows, c_rows, step_rows, state_in)
            gradients = pull_back(grad_rows)
            state_sum, through = local_state(x_heads, b_rows, step_rows, bias_part, rate_part, start_rows)
            return (through[:, None, None] * state_in + state_sum, (gradients, through, state_in))
        _, (first_grads, throughs, states_in) = lax.scan(first_pass, zero_state, (x_blocks, z_blocks, b_blocks, c_blocks, step_blocks, start_blocks, mixed_grads))

        def second_pass(grad_end, block_data):
            x_heads, b_rows, step_rows, start_rows, grad_in, through, state_in = block_data

            def state_part(a_in, b_in, c_in):
                return local_state(a_in, b_in, c_in, bias_part, rate_part, start_rows)
            _, pull_back = jax.vjp(state_part, x_heads, b_rows, step_rows)
            gradients = pull_back((grad_end, lax.optimization_barrier(jnp.sum(grad_end * state_in, axis=(1, 2)))))
            return (grad_in + through[:, None, None] * grad_end, gradients)
        _, second_grads = lax.scan(second_pass, zero_state, (x_blocks, b_blocks, step_blocks, start_blocks, first_grads[5], throughs, states_in), reverse=True)
        grad_x = (first_grads[0] + second_grads[0]).reshape(TOKENS, channel_count).astype(jnp.bfloat16)
        grad_z = first_grads[1].reshape(TOKENS, channel_count).astype(jnp.bfloat16)
        grad_b = (first_grads[2] + second_grads[1]).reshape(TOKENS, group_count * STATE)
        grad_c = first_grads[3].reshape(TOKENS, group_count * STATE)
        grad_maps = jnp.stack([grad_b, grad_c], axis=1).astype(jnp.bfloat16)
        grad_dt = (first_grads[4] + second_grads[2]).reshape(TOKENS, head_count)
        return (grad_x, grad_z, grad_maps, grad_dt)
    results = lax.map(backward_group, group_ids)
    grad_input = jnp.moveaxis(results[0], 0, 1).reshape(TOKENS, HEADS * HEAD_DIM)
    grad_gate = jnp.moveaxis(results[1], 0, 1).reshape(TOKENS, HEADS * HEAD_DIM)
    grad_maps = jnp.moveaxis(results[2], 0, 2).reshape(TOKENS, 2, GROUPS * STATE)
    grad_step = jnp.moveaxis(results[3], 0, 1).reshape(TOKENS, HEADS)
    return (rewards, grad_input, grad_gate, grad_maps, grad_step)
```

```python
import functools

import jax
import jax.numpy as jnp
from jax import lax
from jax.experimental import pallas as pl
from jax.experimental.pallas import tpu as pltpu
from jax.sharding import PartitionSpec as P

STATE = 128
BLK = 128
norm_eps = 1e-05
loss_scale = 64.0
f32 = jnp.float32
bf16 = jnp.bfloat16
VMEM_LIMIT = 24 * 1024 * 1024
STREAM_LIMIT = 52 * 1024 * 1024


def dot(a, b, ca, cb, precision=None):
    return lax.dot_general(
        a, b, (((ca,), (cb,)), ((), ())), precision=precision, preferred_element_type=f32
    )


MSG = f32


def dot_hi_lo(a, b, ca, cb):
    hi = a.astype(bf16)
    lo = (a - hi.astype(f32)).astype(bf16)
    return dot(hi, b, ca, cb) + dot(lo, b, ca, cb)


def rounded(v):
    return lax.reduce_precision(v, exponent_bits=8, mantissa_bits=7)


def split3(v):
    hi = rounded(v)
    mid = rounded(v - hi)
    lo = rounded(v - hi - mid)
    return hi, mid, lo


def split3_in(v):
    hi = v.astype(bf16).astype(f32)
    mid = (v - hi).astype(bf16).astype(f32)
    lo = (v - hi - mid).astype(bf16).astype(f32)
    return hi, mid, lo


def lanes(cols, width):
    rows = cols.shape[0]
    return jnp.concatenate(
        [jnp.broadcast_to(cols[:, h : h + 1], (rows, width)) for h in range(cols.shape[1])], axis=1
    )


def states_kernel(
    groups, off, lens, raw, bias, decay, x, maps, dtg, ag, fg, wg, atg, dttg, segc, segr, s_msg
):
    rows, heads = raw.shape
    hg = heads // groups
    width = x.shape[1] // heads
    v = raw[...] + bias[...]
    dt = jnp.maximum(v, 0.0) + jnp.log1p(jnp.exp(-jnp.abs(v)))
    e = -dt * decay[...]
    r = lax.broadcasted_iota(jnp.int32, (rows, rows), 0)
    c = lax.broadcasted_iota(jnp.int32, (rows, rows), 1)
    tril = (c <= r).astype(f32)
    cum = dot(tril, e, 1, 0, lax.Precision.HIGHEST)
    cum_t = dot(e, tril, 0, 1, lax.Precision.HIGHEST)
    eye = (c == r).astype(f32)
    dt_t = dot(dt, eye, 0, 0, lax.Precision.HIGHEST)
    pos = off[0] + lax.broadcasted_iota(jnp.int32, (rows, 128), 0)
    opening = jnp.int32(0)
    starts = jnp.zeros((rows, 128), f32)
    for k in range(lens.shape[0]):
        starts = jnp.where(pos == opening, 1.0, starts)
        opening = opening + lens[k]
    seg = dot(tril, starts, 1, 0)[:, :1]
    segc[...] = seg
    segr[...] = dot(starts, tril, 0, 1)[:8]
    seg_last = seg[rows - 1 : rows]
    last = cum[rows - 1 : rows]
    w = jnp.where(seg == seg_last, jnp.exp(last - cum), 0.0)
    f = jnp.where(seg == 0.0, jnp.exp(cum), 0.0)
    th = jnp.where(seg_last == 0.0, jnp.exp(last), 0.0)
    wdt = w * dt
    for g in range(groups):
        hs = slice(g * hg, (g + 1) * hg)
        ls = slice(g * hg * width, (g + 1) * hg * width)
        dtg[g] = dt[:, hs]
        ag[g] = cum[:, hs]
        fg[g] = f[:, hs]
        wg[g] = w[:, hs]
        atg[g] = cum_t[hs]
        dttg[g] = dt_t[hs]
        wx = lanes(wdt[:, hs], width) * x[:, ls].astype(f32)
        b_rows = maps[:, g * STATE : (g + 1) * STATE]
        wx_hi = wx.astype(bf16)
        wx_lo = (wx - wx_hi.astype(f32)).astype(bf16)
        s_msg[0:STATE, ls] = (dot(b_rows, wx_hi, 0, 0) + dot(b_rows, wx_lo, 0, 0)).astype(s_msg.dtype)
        if s_msg.dtype == f32:
            s_msg[STATE : STATE + 8, ls] = jnp.broadcast_to(
                lanes(th[:, hs], width), (8, hg * width)
            )
            continue
        hi, mid, lo = split3_in(lanes(th[:, hs], width))
        row = lax.broadcasted_iota(jnp.int32, (16, hg * width), 0)
        tail = jnp.where(row == 0, hi, jnp.where(row == 1, mid, jnp.where(row == 2, lo, 0.0)))
        s_msg[STATE : STATE + 16, ls] = tail.astype(bf16)


def mask_terms(segc, segr, i):
    size = (i + 1) * BLK
    r = i * BLK + lax.broadcasted_iota(jnp.int32, (BLK, size), 0)
    c = lax.broadcasted_iota(jnp.int32, (BLK, size), 1)
    ok = (c <= r) & (segc[i * BLK : (i + 1) * BLK, :] == segr[0:1, :size])
    return jnp.where(ok, 0.0, -1e30)


def within_kernel(x, b, c, dtt, ag, atg, segc, segr, yw, token):
    token[...] = jnp.zeros_like(token)
    rows = x.shape[0]
    hg = ag.shape[2]
    width = x.shape[1] // hg
    for i in range(rows // BLK):
        ti, size = slice(i * BLK, (i + 1) * BLK), (i + 1) * BLK
        scores = dot(c[ti, :], b[:size, :], 1, 1)
        neg = mask_terms(segc, segr, i)
        for h in range(hg):
            decays = jnp.exp(ag[0, ti, h : h + 1] - atg[0, h : h + 1, :size] + neg)
            m = decays * scores * dtt[0, h : h + 1, :size]
            yw[ti, h * width : (h + 1) * width] = dot_hi_lo(
                m, x[:size, h * width : (h + 1) * width], 1, 0
            )


def through_of(rows):
    if rows.dtype == f32:
        return rows[0:1]
    rows = rows.astype(f32)
    return (rows[0:1] + rows[1:2]) + rows[2:3]


def tail_of(through, kind):
    if kind == f32:
        return jnp.broadcast_to(through, (8, through.shape[1]))
    hi, mid, lo = split3_in(through)
    row = lax.broadcasted_iota(jnp.int32, (16, through.shape[1]), 0)
    tail = jnp.where(row == 0, hi, jnp.where(row == 1, mid, jnp.where(row == 2, lo, 0.0)))
    return tail.astype(bf16)


def pair_kernel(forward, place, message, other, out, token):
    core = place[0] % 2
    half = STATE // 2
    late = core if forward else 1 - core
    start = pl.multiple_of(core * half, half)
    mine, theirs = message[pl.ds(start, half), :], other[pl.ds(start, half), :]
    mine, theirs = mine.astype(f32), theirs.astype(f32)
    th_mine, th_theirs = through_of(message[STATE:, :]), through_of(other[STATE:, :])
    is_late = late == 1
    pair = jnp.where(is_late, mine + th_mine * theirs, theirs + th_theirs * mine)
    out[0:half, :] = pair.astype(out.dtype)
    out[half:, :] = tail_of(th_mine * th_theirs, out.dtype)
    token[...] = jnp.zeros_like(token)


def enter_kernel(near, far, out):
    half = STATE // 2
    out[...] = (
        near[0:half, :].astype(f32) + through_of(near[half:, :]) * far[0:half, :].astype(f32)
    ).astype(out.dtype)


def arriving(core, late, own, other, msg):
    half = STATE // 2
    mine, theirs = own[...].astype(f32), other[...].astype(f32)
    low = jnp.where(core == 0, mine, theirs)
    high = jnp.where(core == 0, theirs, mine)
    whole = jnp.concatenate([low, high], axis=0)
    passed = msg[0:STATE, :].astype(f32) + through_of(msg[STATE:, :]) * whole
    return jnp.where(late == 1, passed, whole)


def gate_kernel(place, yw, x, z, c, fg, own, other, msg, skip, gain, u, y, mixed, along, s_in):
    width = x.shape[1] // fg.shape[2]
    state = arriving(place[0] % 2, place[0] % 2, own, other, msg)
    s_hi = state.astype(bf16)
    s_lo = (state - s_hi.astype(f32)).astype(bf16)
    s_in[...] = s_hi
    out = (
        yw[...]
        + lanes(fg[0], width) * (dot(c[...], s_hi, 1, 0) + dot(c[...], s_lo, 1, 0))
        + skip[...] * x[...].astype(f32)
    )
    y[...] = out
    zf = z[...].astype(f32)
    gated = out * zf / (1.0 + jnp.exp(-zf))
    mean = jnp.mean(gated * gated, axis=1, keepdims=True)
    rows16 = (gated * lax.rsqrt(mean + norm_eps) * gain[...]).astype(bf16)
    mixed[...] = rows16
    part = jnp.sum(rows16.astype(f32) * u[...], axis=1, keepdims=True)

    @pl.when(pl.program_id(0) == 0)
    def _():
        along[...] = part

    @pl.when(pl.program_id(0) > 0)
    def _():
        along[...] += part


def gate_back_kernel(dm, u, p1, p2, y, z, gain, c, fg, th, grad_z, dy, g_state):
    width = z.shape[1] // fg.shape[2]
    d_mixed = p1[...] * u[...] - p2[...] * dm[...]
    zf = z[...].astype(f32)
    sig = 1.0 / (1.0 + jnp.exp(-zf))
    silu = zf * sig
    yv = y[...]
    gated = yv * silu
    inv = lax.rsqrt(jnp.mean(gated * gated, axis=1, keepdims=True) + norm_eps)
    dn = d_mixed * gain[...]
    corr = jnp.mean(dn * gated, axis=1, keepdims=True)
    dgated = inv * dn - gated * (inv * inv * inv * corr)
    grad_z[...] = (dgated * yv * (sig * (1.0 + zf * (1.0 - sig)))).astype(bf16)
    dyv = (dgated * silu).astype(bf16)
    dy[...] = dyv
    fdy = (lanes(fg[0], width) * dyv.astype(f32)).astype(bf16)
    g_state[0:STATE, :] = dot(c[...], fdy, 0, 0).astype(bf16)
    g_state[STATE:, :] = tail_of(th[...], bf16)


def within_back_kernel(
    x, b, c, dtg, ag, atg, fg, segc, segr, dy, s_in, dxd, dc, db, token
):
    rows = x.shape[0]
    hg = dtg.shape[2]
    width = x.shape[1] // hg
    xd = (lanes(dtg[0], width) * x[...].astype(f32)).astype(bf16)
    dyv = dy[...]
    fdy = (lanes(fg[0], width) * dyv.astype(f32)).astype(bf16)
    token[...] = jnp.zeros_like(token)
    carried = dot(fdy, s_in[...], 1, 1)
    for i in range(rows // BLK):
        ti, size = slice(i * BLK, (i + 1) * BLK), (i + 1) * BLK
        scores = dot(c[ti, :], b[:size, :], 1, 1)
        neg = mask_terms(segc, segr, i)
        total = jnp.zeros((BLK, size), f32)
        for h in range(hg):
            ls = slice(h * width, (h + 1) * width)
            decays = jnp.exp(ag[0, ti, h : h + 1] - atg[0, h : h + 1, :size] + neg)
            m = (decays * scores).astype(bf16)
            total = total + decays * dot(dyv[ti, ls], xd[:size, ls], 1, 1)
            back = dot(m, dyv[ti, ls], 0, 0)
            if i > 0:
                dxd[: i * BLK, ls] += back[: i * BLK]
            dxd[ti, ls] = back[i * BLK :]
        dgv = total.astype(bf16)
        dc[ti, :] = (carried[ti] + dot(dgv, b[:size, :], 1, 0)).astype(bf16)
        back = dot(dgv, c[ti, :], 0, 0)
        if i > 0:
            db[: i * BLK, :] += back[: i * BLK]
        db[ti, :] = back[i * BLK :]


def final_kernel(
    place, own, other, msg, s_in, s_loc, th, x, b, dy, y, dxd, dbp, dtg, wg, skip, grad_x, db, grad_dt, d_cum
):
    hg = dtg.shape[2]
    rows = x.shape[0]
    width = x.shape[1] // hg
    xf = x[...].astype(f32)
    dyv = dy[...].astype(f32)
    dtl = lanes(dtg[0], width)
    wl = lanes(wg[0], width)
    core = place[0] % 2
    dsv = arriving(core, 1 - core, own, other, msg).astype(bf16)
    bds = dot(b[...], dsv, 1, 0)
    wx = (wl * dtl * xf).astype(bf16)
    db[...] = (dbp[...] + dot(wx, dsv, 1, 1)).astype(bf16)
    q = dxd[...] + wl * bds
    grad_x[...] = (dtl * q + skip[...] * dyv).astype(bf16)
    xd = (dtl * xf).astype(bf16).astype(f32)
    direct = xf * q
    cums = dyv * (y[...] - skip[...] * xf) - xd * dxd[...] - wx.astype(f32) * bds
    ends = dsv.astype(f32) * (
        th[...] * s_in[...].astype(f32) + s_loc[...].astype(f32)
    )
    last = lax.broadcasted_iota(jnp.int32, (rows, 1), 0) == rows - 1
    for h in range(hg):
        ls = slice(h * width, (h + 1) * width)
        grad_dt[0, :, h : h + 1] = jnp.sum(direct[:, ls], axis=1, keepdims=True)
        end = jnp.sum(jnp.sum(ends[:, ls], axis=0, keepdims=True), axis=1, keepdims=True)
        d_cum[0, :, h : h + 1] = jnp.sum(cums[:, ls], axis=1, keepdims=True) + jnp.where(
            last, end, 0.0
        )


def step_kernel(groups, raw, bias, decay, grad_dt, d_cum, out):
    rows, heads = raw.shape
    r = lax.broadcasted_iota(jnp.int32, (rows, rows), 0)
    c = lax.broadcasted_iota(jnp.int32, (rows, rows), 1)
    triu = (c >= r).astype(f32)
    direct = jnp.concatenate([grad_dt[g] for g in range(groups)], axis=1)
    dcv = jnp.concatenate([d_cum[g] for g in range(groups)], axis=1)
    de = dot(triu, dcv, 1, 0, lax.Precision.HIGHEST)
    v = raw[...] + bias[...]
    out[...] = (direct - decay[...] * de) / (1.0 + jnp.exp(-v))


def head_kernel(rows3, w, out, token):
    token[...] = jnp.zeros_like(token)

    @pl.when(pl.program_id(0) == 0)
    def _():
        out[...] = jnp.zeros_like(out)

    both = dot(rows3[...], w[...], 1, 0)
    out[...] += (both[0:1] + both[1:2]) + both[2:3]


def project_kernel(mixed, w, out, token):
    out[...] = dot(mixed[...], w[...], 1, 1).astype(bf16)
    token[...] = jnp.zeros_like(token)


def in_lanes(column):
    hi, mid, lo = split3_in(column)
    lane = lax.broadcasted_iota(jnp.int32, (column.shape[0], 128), 1)
    return jnp.where(
        lane == 0, hi, jnp.where(lane == 1, mid, jnp.where(lane == 2, lo, 0.0))
    ).astype(bf16)


def from_lanes(tile):
    tile = tile.astype(f32)
    return (tile[:, 0:1] + tile[:, 1:2]) + tile[:, 2:3]


def project_first_kernel(mixed, column, w, out, token):
    size = w.shape[0]
    out[:, :size] = dot(mixed[...], w[...], 1, 1).astype(bf16)
    out[:, size:] = in_lanes(column[...])
    token[...] = jnp.zeros_like(token)


def add_kernel(size, a, b, out, token):
    out[:, :size] = (a[:, :size].astype(f32) + b[:, :size].astype(f32)).astype(bf16)
    if size < a.shape[1]:
        out[:, size:] = in_lanes(from_lanes(a[:, size:]) + from_lanes(b[:, size:]))
    token[...] = jnp.zeros_like(token)


def choose_kernel(size, place, total, got, *refs):
    middle = (place[0] == 1) | (place[0] == 2)
    h = jnp.where(middle, total[:, :size].astype(f32), got[:, :size].astype(f32))
    square = jnp.sum(h * h, axis=1, keepdims=True)
    if size < total.shape[1]:
        hidden, squares, token, along = refs
        along[...] = jnp.where(middle, from_lanes(total[:, size:]), from_lanes(got[:, size:]))
    else:
        before, hidden, squares, token = refs
        square = before[...] + square
    hidden[...] = h.astype(bf16)
    squares[...] = square
    token[...] = jnp.zeros_like(token)


def back_kernel(first, hidden, w, *refs):
    before, out, token = (None,) + refs if first else refs
    token[...] = jnp.zeros_like(token)
    value = dot(hidden[...], w[...], 1, 0)
    out[...] = value if first else before[...] + value


def partner_kernel(off, pairs, out):
    rows, total = out.shape[0], pairs.shape[1]
    v = jnp.broadcast_to(pairs[...].astype(f32), (8, total))
    even = lax.broadcasted_iota(jnp.int32, (8, total), 1) % 2 == 0
    signed = jnp.where(even, -1.0 - pltpu.roll(v, total - 1, 1), 1.0 + pltpu.roll(v, 1, 1))
    tokens = (off[0] + lax.broadcasted_iota(jnp.int32, (rows, 1), 0)).astype(f32)
    acc = jnp.zeros((rows, 128), f32)
    for k in range(total // 128):
        ls = slice(k * 128, (k + 1) * 128)
        acc = acc + jnp.where(tokens == v[0:1, ls], signed[0:1, ls], 0.0)
    out[...] = jnp.sum(acc, axis=1, keepdims=True)


def vmem():
    return pl.BlockSpec(memory_space=pltpu.VMEM)


def smem():
    return pl.BlockSpec(memory_space=pltpu.SMEM)


def token_spec():
    return pl.BlockSpec((8, 128), lambda *at: (0, 0))


def call(
    kernel, grid, ins, outs, shapes, after=(), aliases=None, flops=0, size=0, limit=VMEM_LIMIT
):
    count = len(after)
    inner = (lambda *refs: kernel(*refs[count:])) if count else kernel
    run = pl.pallas_call(
        inner,
        grid=grid,
        in_specs=[pl.BlockSpec(memory_space=pl.ANY)] * count + list(ins),
        out_specs=outs,
        out_shape=shapes,
        input_output_aliases={k + count: v for k, v in (aliases or {}).items()},
        compiler_params=pltpu.CompilerParams(vmem_limit_bytes=limit),
        cost_estimate=pl.CostEstimate(flops=flops, bytes_accessed=size, transcendentals=0),
    )
    return lambda *args: run(*after, *args)


def shape(dims, kind):
    return jax.ShapeDtypeStruct(dims, kind)


TOKEN = (8, 128)


def hops(count, distance):
    return [(i, i + distance) for i in range(count) if 0 <= i + distance < count]


def chain(message, forward, beside):
    count, place = lax.axis_size("seq"), lax.axis_index("seq").reshape(1)
    kind = message.dtype
    half = STATE // 2
    swap = [(i, i ^ 1) for i in range(count)]
    other = lax.ppermute(message, "seq", swap)
    pair_rows = half + message.shape[0] - STATE
    pair, token = call(
        functools.partial(pair_kernel, forward),
        (),
        [smem(), vmem(), vmem()],
        [vmem(), vmem()],
        [shape((pair_rows, message.shape[1]), kind), shape(TOKEN, f32)],
    )(place, message, other)
    way = 1 if forward else -1
    near = lax.ppermute(pair, "seq", hops(count, 2 * way))
    far = lax.ppermute(pair, "seq", hops(count, 4 * way))
    results, tokens = beside(token)
    own = call(
        enter_kernel,
        (),
        [vmem(), vmem()],
        vmem(),
        shape((half, message.shape[1]), kind),
        after=tokens,
    )(near, far)
    return own, lax.ppermute(own, "seq", swap), other, results


def pieces(count):
    unit = count // 8
    return [
        (0, unit),
        (unit, unit),
        (2 * unit, 2 * unit),
        (4 * unit, 2 * unit),
        (6 * unit, unit),
        (7 * unit, unit),
    ]


def hidden_products(mixed, along, out_weight):
    count, place = lax.axis_size("tensor"), lax.axis_index("tensor").reshape(1)
    rows, channels = mixed.shape
    model_width = out_weight.shape[0]
    plan = pieces(model_width)
    line = count == 4
    tile = min(512, channels)

    def project(base, size, column=None):
        step = min(size, 512)
        with_column = column is not None
        wide = size + 128 if with_column else size
        column_spec = pl.BlockSpec((rows, 1), lambda j: (0, 0))
        ins = [
            pl.BlockSpec((rows, channels), lambda j: (0, 0)),
            pl.BlockSpec((step, channels), lambda j: (base // step + j, 0)),
        ]
        return call(
            project_first_kernel if with_column else project_kernel,
            (size // step,),
            [ins[0], column_spec, ins[1]] if with_column else ins,
            [
                pl.BlockSpec((rows, wide if with_column else step), lambda j: (0, j)),
                token_spec(),
            ],
            [shape((rows, wide), bf16), shape(TOKEN, f32)],
            flops=2 * rows * channels * size,
            size=2 * channels * size,
            limit=STREAM_LIMIT,
        )(*((mixed, column, out_weight) if with_column else (mixed, out_weight)))

    def add(size, a, b, after):
        return call(
            functools.partial(add_kernel, size),
            (),
            [vmem(), vmem()],
            [vmem(), vmem()],
            [shape(a.shape, bf16), shape(TOKEN, f32)],
            after=after,
            size=6 * a.size,
        )(a, b)

    def choose(size, total, got, squares, after):
        first = size < total.shape[1]
        column = shape((rows, 1), f32)
        return call(
            functools.partial(choose_kernel, size),
            (),
            [smem()] + [vmem()] * (2 if first else 3),
            [vmem()] * (4 if first else 3),
            [shape((rows, size), bf16), column, shape(TOKEN, f32)] + [column] * first,
            after=after,
            size=6 * total.size,
        )(*((place, total, got) if first else (place, total, got, squares)))

    def back(hidden, base, size, before, after):
        first = before is None
        wide = pl.BlockSpec((rows, tile), lambda j: (0, j))
        ins = [
            pl.BlockSpec((rows, size), lambda j: (0, 0)),
            pl.BlockSpec((size, tile), lambda j: (base // size, j)),
        ]
        return call(
            functools.partial(back_kernel, first),
            (channels // tile,),
            ins if first else ins + [wide],
            [wide, token_spec()],
            [shape((rows, channels), f32), shape(TOKEN, f32)],
            after=after,
            aliases=None if first else {2: 0},
            flops=2 * rows * channels * size,
            size=2 * channels * size + 8 * rows * channels,
            limit=STREAM_LIMIT,
        )(*((hidden, out_weight) if first else (hidden, out_weight, before)))

    squares = jnp.zeros((rows, 1), f32)
    dm = None
    if not line:
        along = lax.psum(along, "tensor")
        for base, size in plan:
            h = lax.psum(project(base, size)[0].astype(f32), "tensor").astype(bf16)
            squares = squares + jnp.sum(jnp.square(h.astype(f32)), axis=1, keepdims=True)
            dm, _ = back(h, base, size, dm, ())
        return dm, squares, along
    outward, across, inward = [(1, 0), (2, 3)], [(1, 2), (2, 1)], [(0, 1), (3, 2)]
    own, moved = [], []
    for base, size in plan:
        part, token = project(base, size, None if own else along)
        own.append(part)
        moved.append(lax.ppermute(part, "tensor", inward))
    sums, crossed, totals, got = {}, {}, {}, {}
    after = (token,)
    last = len(plan) - 1
    for slot in range(len(plan) + 2):
        k = slot
        if k <= last:
            sums[k], token = add(plan[k][1], own[k], moved[k], after)
            crossed[k] = lax.ppermute(sums[k], "tensor", across)
            after = (token,)
        k = slot - 1
        if 0 <= k <= last:
            totals[k], token = add(plan[k][1], sums[k], crossed[k], after)
            got[k] = lax.ppermute(totals[k], "tensor", outward)
            after = (token,)
        k = slot - 2
        if 0 <= k <= last:
            h, squares, token, *column = choose(plan[k][1], totals[k], got[k], squares, after)
            along = column[0] if column else along
            dm, token = back(h, *plan[k], dm, (token,))
            after = (token,)
    return dm, squares, along


def picked_rewards(rewards, partner):
    rows = rewards.shape[0]
    count, place = lax.axis_size("seq"), lax.axis_index("seq")
    flat = rewards.reshape(rows)
    other = lax.ppermute(flat, "seq", [(i, i ^ 1) for i in range(count)])
    even = place % 2 == 0
    both = jnp.concatenate([jnp.where(even, flat, other), jnp.where(even, other, flat)])
    total = jnp.zeros((rows, 1), f32)
    for d in range(count // 2):
        seen = both
        if d:
            seen = lax.ppermute(both, "seq", [(i, i ^ (2 * d)) for i in range(count)])
        base = ((place // 2) ^ d) * 2 * rows
        at = (base + jnp.arange(2 * rows, dtype=jnp.int32)).astype(f32)
        total = total + jnp.sum(
            jnp.where(partner == at[None, :], seen[None, :], 0.0), axis=1, keepdims=True
        )
    return total


def on_device(
    ssd_input,
    gate_input,
    state_maps,
    step_raw,
    step_bias,
    decay_rate,
    skip_gain,
    norm_gain,
    out_weight,
    reward_head,
    traj_lengths,
    step_pairs,
):
    rows, channels = ssd_input.shape
    heads = step_raw.shape[1]
    width = channels // heads
    groups = state_maps.shape[2] // STATE
    hg = heads // groups
    gw = hg * width
    model_width = out_weight.shape[0]
    offset = lax.axis_index("seq") * rows
    maps = state_maps.reshape(rows, 2 * groups * STATE)
    bias2, decay2 = step_bias[None, :], decay_rate[None, :]
    skip = jnp.repeat(skip_gain, width)[None, :]
    gain = norm_gain[None, :]

    cols = pl.BlockSpec((rows, gw), lambda g: (0, g))
    row1 = pl.BlockSpec((1, gw), lambda g: (0, g))
    b_spec = pl.BlockSpec((rows, STATE), lambda g: (0, g))
    c_spec = pl.BlockSpec((rows, STATE), lambda g: (0, groups + g))
    state = pl.BlockSpec((STATE, gw), lambda g: (0, g))
    per_g = pl.BlockSpec((1, rows, hg), lambda g: (g, 0, 0))
    per_gt = pl.BlockSpec((1, hg, rows), lambda g: (g, 0, 0))
    segc_spec = pl.BlockSpec((rows, 1), lambda g: (0, 0))
    segr_spec = pl.BlockSpec((8, rows), lambda g: (0, 0))
    grp = shape((groups, rows, hg), f32)

    dtg, ag, fg, wg, atg, dttg, segc, segr, s_msg = call(
        functools.partial(states_kernel, groups),
        (),
        [smem(), smem(), vmem(), vmem(), vmem(), vmem(), vmem()],
        [vmem()] * 9,
        [
            grp,
            grp,
            grp,
            grp,
            shape((groups, hg, rows), f32),
            shape((groups, hg, rows), f32),
            shape((rows, 1), f32),
            shape((8, rows), f32),
            shape((STATE + 16 if MSG == bf16 else STATE + 8, channels), MSG),
        ],
    )(offset.reshape(1), traj_lengths, step_raw, bias2, decay2, ssd_input, maps)

    place = lax.axis_index("seq").reshape(1)
    th = s_msg[STATE : STATE + 1]
    head_rows = jnp.concatenate(
        list(split3(reward_head[None, :])) + [jnp.zeros((13, model_width), f32)], axis=0
    ).astype(bf16)
    total = step_pairs.shape[0]

    def beside_forward(token):
        yw, t1 = call(
            within_kernel,
            (groups,),
            [cols, b_spec, c_spec, per_gt, per_g, per_gt, segc_spec, segr_spec],
            [cols, token_spec()],
            [shape((rows, channels), f32), shape(TOKEN, f32)],
            after=(token,),
            flops=2 * rows * rows * channels,
            size=8 * rows * channels,
        )(ssd_input, maps, maps, dttg, ag, atg, segc, segr)
        step = model_width // 8
        u, t2 = call(
            head_kernel,
            (8,),
            [
                pl.BlockSpec((16, step), lambda j: (0, j)),
                pl.BlockSpec((step, channels), lambda j: (j, 0)),
            ],
            [pl.BlockSpec((1, channels), lambda j: (0, 0)), token_spec()],
            [shape((1, channels), f32), shape(TOKEN, f32)],
            after=(t1,),
            size=2 * model_width * channels,
            limit=STREAM_LIMIT,
        )(head_rows, out_weight)
        found = call(
            partner_kernel,
            (),
            [smem(), vmem()],
            vmem(),
            shape((rows, 1), f32),
            after=(t2,),
        )(offset.reshape(1), step_pairs.reshape(1, total))
        return (yw, u, found), (t2, found)

    own_s, other_s, other_msg, (yw, u, found) = chain(s_msg, True, beside_forward)
    partner = jnp.abs(found) - 1.0
    side = jnp.where(found < 0, -1.0, 1.0)

    tail = s_msg.shape[0]
    half_spec = pl.BlockSpec((STATE // 2, gw), lambda g: (0, g))
    y, mixed, along_part, s_in = call(
        gate_kernel,
        (groups,),
        [
            smem(),
            cols,
            cols,
            cols,
            c_spec,
            per_g,
            half_spec,
            half_spec,
            pl.BlockSpec((tail, gw), lambda g: (0, g)),
            row1,
            row1,
            row1,
        ],
        [cols, cols, pl.BlockSpec((rows, 1), lambda g: (0, 0)), state],
        [
            shape((rows, channels), f32),
            shape((rows, channels), bf16),
            shape((rows, 1), f32),
            shape((STATE, channels), bf16),
        ],
        flops=2 * rows * STATE * channels,
        size=14 * rows * channels,
    )(
        place,
        yw,
        ssd_input,
        gate_input,
        maps,
        fg,
        own_s,
        other_s,
        other_msg,
        skip,
        gain,
        u,
    )

    dm, squares, along = hidden_products(mixed, along_part, out_weight)
    scale = jnp.sqrt(squares / model_width + norm_eps)
    rewards = along / scale
    picked = picked_rewards(rewards, partner)
    push = loss_scale * jax.nn.sigmoid(side * (rewards - picked))
    own_grad = side * push
    p1 = own_grad / scale
    p2 = own_grad * along / (model_width * scale * scale * scale)

    grad_gate, dy, g_state = call(
        gate_back_kernel,
        (groups,),
        [cols, row1, segc_spec, segc_spec, cols, cols, row1, c_spec, per_g, row1],
        [cols, cols, pl.BlockSpec((STATE + 16, gw), lambda g: (0, g))],
        [
            shape((rows, channels), bf16),
            shape((rows, channels), bf16),
            shape((STATE + 16, channels), bf16),
        ],
        flops=2 * rows * STATE * channels,
        size=14 * rows * channels,
    )(dm, u, p1, p2, y, gate_input, gain, maps, fg, th)

    def beside_back(token):
        dxd, dc, dbp, t1 = call(
            within_back_kernel,
            (groups,),
            [
                cols,
                b_spec,
                c_spec,
                per_g,
                per_g,
                per_gt,
                per_g,
                segc_spec,
                segr_spec,
                cols,
                state,
            ],
            [cols, b_spec, b_spec, token_spec()],
            [
                shape((rows, channels), f32),
                shape((rows, groups * STATE), bf16),
                shape((rows, groups * STATE), f32),
                shape(TOKEN, f32),
            ],
            after=(token,),
            flops=4 * rows * rows * channels,
            size=10 * rows * channels,
        )(ssd_input, maps, maps, dtg, ag, atg, fg, segc, segr, dy, s_in)
        return (dxd, dc, dbp), (t1,)

    own_d, other_d, other_g, (dxd, dc, dbp) = chain(g_state, False, beside_back)

    grad_input, db, grad_dt, d_cum = call(
        final_kernel,
        (groups,),
        [
            smem(),
            half_spec,
            half_spec,
            pl.BlockSpec((STATE + 16, gw), lambda g: (0, g)),
            state,
            state,
            row1,
            cols,
            b_spec,
            cols,
            cols,
            cols,
            b_spec,
            per_g,
            per_g,
            row1,
        ],
        [cols, b_spec, per_g, per_g],
        [
            shape((rows, channels), bf16),
            shape((rows, groups * STATE), bf16),
            grp,
            grp,
        ],
        flops=4 * rows * STATE * channels,
        size=16 * rows * channels,
    )(
        place,
        own_d,
        other_d,
        other_g,
        s_in,
        s_msg,
        th,
        ssd_input,
        maps,
        dy,
        y,
        dxd,
        dbp,
        dtg,
        wg,
        skip,
    )
    grad_step = call(
        functools.partial(step_kernel, groups),
        (),
        [vmem()] * 5,
        vmem(),
        shape((rows, heads), f32),
    )(step_raw, bias2, decay2, grad_dt, d_cum)
    grad_maps = jnp.stack([db, dc], axis=1)
    return (rewards.reshape(rows), grad_input, grad_gate, grad_maps, grad_step)


def solution(mesh):
    return jax.shard_map(
        on_device,
        mesh=mesh,
        in_specs=(
            P("seq", "tensor"),
            P("seq", "tensor"),
            P("seq", None, "tensor"),
            P("seq", "tensor"),
            P("tensor"),
            P("tensor"),
            P("tensor"),
            P("tensor"),
            P(None, "tensor"),
            P(),
            P(),
            P(),
        ),
        out_specs=(
            P("seq"),
            P("seq", "tensor"),
            P("seq", "tensor"),
            P("seq", None, "tensor"),
            P("seq", "tensor"),
        ),
        check_vma=False,
    )
```

```python
import functools

import jax
import jax.numpy as jnp
from jax import lax
from jax.experimental import pallas as pl
from jax.experimental.pallas import tpu as pltpu
from jax.sharding import PartitionSpec as P

STATE = 128
BLK = 128
norm_eps = 1e-05
loss_scale = 64.0
f32 = jnp.float32
bf16 = jnp.bfloat16
VMEM_LIMIT = 24 * 1024 * 1024
STREAM_LIMIT = 49 * 1024 * 1024


def dot(a, b, ca, cb, precision=None):
    return lax.dot_general(
        a, b, (((ca,), (cb,)), ((), ())), precision=precision, preferred_element_type=f32
    )


MSG = f32


def dot_hi_lo(a, b, ca, cb):
    hi = a.astype(bf16)
    lo = (a - hi.astype(f32)).astype(bf16)
    return dot(hi, b, ca, cb) + dot(lo, b, ca, cb)


def rounded(v):
    return lax.reduce_precision(v, exponent_bits=8, mantissa_bits=7)


def split3(v):
    hi = rounded(v)
    mid = rounded(v - hi)
    lo = rounded(v - hi - mid)
    return hi, mid, lo


def split3_in(v):
    hi = v.astype(bf16).astype(f32)
    mid = (v - hi).astype(bf16).astype(f32)
    lo = (v - hi - mid).astype(bf16).astype(f32)
    return hi, mid, lo


def lanes(cols, width):
    rows = cols.shape[0]
    return jnp.concatenate(
        [jnp.broadcast_to(cols[:, h : h + 1], (rows, width)) for h in range(cols.shape[1])], axis=1
    )


def states_kernel(
    groups, off, lens, raw, bias, decay, x, maps, packed, atg, dttg, segc, segr, s_msg
):
    rows, heads = raw.shape
    hg = heads // groups
    width = x.shape[1] // heads
    v = raw[...] + bias[...]
    dt = jnp.maximum(v, 0.0) + jnp.log1p(jnp.exp(-jnp.abs(v)))
    e = -dt * decay[...]
    r = lax.broadcasted_iota(jnp.int32, (rows, rows), 0)
    c = lax.broadcasted_iota(jnp.int32, (rows, rows), 1)
    tril = (c <= r).astype(f32)
    cum = dot(tril, e, 1, 0, lax.Precision.HIGHEST)
    cum_t = dot(e, tril, 0, 1, lax.Precision.HIGHEST)
    eye = (c == r).astype(f32)
    dt_t = dot(dt, eye, 0, 0, lax.Precision.HIGHEST)
    pos = off[0] + lax.broadcasted_iota(jnp.int32, (rows, 128), 0)
    opening = jnp.int32(0)
    starts = jnp.zeros((rows, 128), f32)
    for k in range(lens.shape[0]):
        starts = jnp.where(pos == opening, 1.0, starts)
        opening = opening + lens[k]
    seg = dot(tril, starts, 1, 0)[:, :1]
    segc[...] = seg
    segr[...] = dot(starts, tril, 0, 1)[:8]
    seg_last = seg[rows - 1 : rows]
    last = cum[rows - 1 : rows]
    w = jnp.where(seg == seg_last, jnp.exp(last - cum), 0.0)
    f = jnp.where(seg == 0.0, jnp.exp(cum), 0.0)
    th = jnp.where(seg_last == 0.0, jnp.exp(last), 0.0)
    wdt = w * dt
    fill = jnp.zeros((rows, 128 - 4 * heads), f32)
    packed[...] = jnp.concatenate([dt, cum, f, w, fill], axis=1)
    for g in range(groups):
        hs = slice(g * hg, (g + 1) * hg)
        ls = slice(g * hg * width, (g + 1) * hg * width)
        atg[g] = cum_t[hs]
        dttg[g] = dt_t[hs]
        wx = lanes(wdt[:, hs], width) * x[:, ls].astype(f32)
        b_rows = maps[:, g * STATE : (g + 1) * STATE]
        wx_hi = wx.astype(bf16)
        wx_lo = (wx - wx_hi.astype(f32)).astype(bf16)
        s_msg[0:STATE, ls] = (dot(b_rows, wx_hi, 0, 0) + dot(b_rows, wx_lo, 0, 0)).astype(s_msg.dtype)
        if s_msg.dtype == f32:
            s_msg[STATE : STATE + 8, ls] = jnp.broadcast_to(
                lanes(th[:, hs], width), (8, hg * width)
            )
            continue
        hi, mid, lo = split3_in(lanes(th[:, hs], width))
        row = lax.broadcasted_iota(jnp.int32, (16, hg * width), 0)
        tail = jnp.where(row == 0, hi, jnp.where(row == 1, mid, jnp.where(row == 2, lo, 0.0)))
        s_msg[STATE : STATE + 16, ls] = tail.astype(bf16)


def head_columns(packed, heads, count):
    shift = (128 - count * pl.program_id(0)) % 128
    turned = pltpu.roll(packed[...], shift, 1)
    return [turned[:, k * heads : k * heads + count] for k in range(4)]


def mask_terms(segc, segr, i):
    size = (i + 1) * BLK
    r = i * BLK + lax.broadcasted_iota(jnp.int32, (BLK, size), 0)
    c = lax.broadcasted_iota(jnp.int32, (BLK, size), 1)
    ok = (c <= r) & (segc[i * BLK : (i + 1) * BLK, :] == segr[0:1, :size])
    return jnp.where(ok, 0.0, -1e30)


def within_kernel(heads, x, b, c, dtt, packed, atg, segc, segr, yw, token):
    token[...] = jnp.zeros_like(token)
    rows = x.shape[0]
    hg = atg.shape[1]
    _, cum, _, _ = head_columns(packed, heads, hg)
    width = x.shape[1] // hg
    for i in range(rows // BLK):
        ti, size = slice(i * BLK, (i + 1) * BLK), (i + 1) * BLK
        scores = dot(c[ti, :], b[:size, :], 1, 1)
        neg = mask_terms(segc, segr, i)
        for h in range(hg):
            decays = jnp.exp(cum[ti, h : h + 1] - atg[0, h : h + 1, :size] + neg)
            m = decays * scores * dtt[0, h : h + 1, :size]
            yw[ti, h * width : (h + 1) * width] = dot_hi_lo(
                m, x[:size, h * width : (h + 1) * width], 1, 0
            )


def sum3(rows):
    rows = rows.astype(f32)
    return (rows[0:1] + rows[1:2]) + rows[2:3]


def through_of(rows):
    if rows.dtype == f32:
        return rows[0:1]
    return sum3(rows)


def tail_of(through, kind):
    if kind == f32:
        return jnp.broadcast_to(through, (8, through.shape[1]))
    hi, mid, lo = split3_in(through)
    row = lax.broadcasted_iota(jnp.int32, (16, through.shape[1]), 0)
    tail = jnp.where(row == 0, hi, jnp.where(row == 1, mid, jnp.where(row == 2, lo, 0.0)))
    return tail.astype(bf16)


def pair_kernel(forward, place, message, other, out, far, token):
    core = place[0] % 2
    half = STATE // 2
    late = core if forward else 1 - core
    start = pl.multiple_of(core * half, half)
    mine, theirs = message[pl.ds(start, half), :], other[pl.ds(start, half), :]
    mine, theirs = mine.astype(f32), theirs.astype(f32)
    th_mine, th_theirs = through_of(message[STATE:, :]), through_of(other[STATE:, :])
    is_late = late == 1
    pair = jnp.where(is_late, mine + th_mine * theirs, theirs + th_theirs * mine)
    out[0:half, :] = pair.astype(out.dtype)
    out[half:, :] = tail_of(th_mine * th_theirs, out.dtype)
    far[...] = pair.astype(bf16)
    token[...] = jnp.zeros_like(token)


def enter_kernel(near, far, out):
    half = STATE // 2
    out[...] = (
        near[0:half, :].astype(f32) + through_of(near[half:, :]) * far[...].astype(f32)
    ).astype(out.dtype)


def arriving(core, late, own, other, msg):
    half = STATE // 2
    mine, theirs = own[...].astype(f32), other[...].astype(f32)
    low = jnp.where(core == 0, mine, theirs)
    high = jnp.where(core == 0, theirs, mine)
    whole = jnp.concatenate([low, high], axis=0)
    passed = msg[0:STATE, :].astype(f32) + through_of(msg[STATE:, :]) * whole
    return jnp.where(late == 1, passed, whole)


def gate_kernel(
    heads, hg, place, yw, x, z, c, packed, own, other, msg, skip, gain, y, mixed, s_in
):
    width = x.shape[1] // hg
    _, _, f, _ = head_columns(packed, heads, hg)
    state = arriving(place[0] % 2, place[0] % 2, own, other, msg)
    s_hi = state.astype(bf16)
    s_lo = (state - s_hi.astype(f32)).astype(bf16)
    s_in[...] = s_hi
    out = (
        yw[...]
        + lanes(f, width) * (dot(c[...], s_hi, 1, 0) + dot(c[...], s_lo, 1, 0))
        + skip[...] * x[...].astype(f32)
    )
    y[...] = out
    zf = z[...].astype(f32)
    gated = out * zf / (1.0 + jnp.exp(-zf))
    mean = jnp.mean(gated * gated, axis=1, keepdims=True)
    mixed[...] = (gated * lax.rsqrt(mean + norm_eps) * gain[...]).astype(bf16)


def gate_back_kernel(
    heads, hg, dm, hidden, w, p1, p2, y, z, gain, c, packed, th, grad_z, dy, g_state
):
    rows = z.shape[0]
    width = z.shape[1] // hg
    _, _, f, _ = head_columns(packed, heads, hg)
    products = dm[...] + dot(hidden[...], w[...], 1, 0)
    d_mixed = p1[...] * sum3(products[rows:]) - p2[...] * products[:rows]
    zf = z[...].astype(f32)
    sig = 1.0 / (1.0 + jnp.exp(-zf))
    silu = zf * sig
    yv = y[...]
    gated = yv * silu
    inv = lax.rsqrt(jnp.mean(gated * gated, axis=1, keepdims=True) + norm_eps)
    dn = d_mixed * gain[...]
    corr = jnp.mean(dn * gated, axis=1, keepdims=True)
    dgated = inv * dn - gated * (inv * inv * inv * corr)
    grad_z[...] = (dgated * yv * (sig * (1.0 + zf * (1.0 - sig)))).astype(bf16)
    dyv = (dgated * silu).astype(bf16)
    dy[...] = dyv
    fdy = (lanes(f, width) * dyv.astype(f32)).astype(bf16)
    g_state[0:STATE, :] = dot(c[...], fdy, 0, 0).astype(bf16)
    g_state[STATE:, :] = tail_of(th[...], bf16)


def within_back_kernel(
    heads, x, b, c, packed, atg, segc, segr, dy, s_in, dxd, dc, db, token
):
    rows = x.shape[0]
    hg = atg.shape[1]
    width = x.shape[1] // hg
    dt, cum, f, _ = head_columns(packed, heads, hg)
    xd = (lanes(dt, width) * x[...].astype(f32)).astype(bf16)
    dyv = dy[...]
    fdy = (lanes(f, width) * dyv.astype(f32)).astype(bf16)
    token[...] = jnp.zeros_like(token)
    carried = dot(fdy, s_in[...], 1, 1)
    for i in range(rows // BLK):
        ti, size = slice(i * BLK, (i + 1) * BLK), (i + 1) * BLK
        scores = dot(c[ti, :], b[:size, :], 1, 1)
        neg = mask_terms(segc, segr, i)
        total = jnp.zeros((BLK, size), f32)
        for h in range(hg):
            ls = slice(h * width, (h + 1) * width)
            decays = jnp.exp(cum[ti, h : h + 1] - atg[0, h : h + 1, :size] + neg)
            m = (decays * scores).astype(bf16)
            total = total + decays * dot(dyv[ti, ls], xd[:size, ls], 1, 1)
            back = dot(m, dyv[ti, ls], 0, 0)
            if i > 0:
                dxd[: i * BLK, ls] += back[: i * BLK]
            dxd[ti, ls] = back[i * BLK :]
        dgv = total.astype(bf16)
        dc[ti, :] = (carried[ti] + dot(dgv, b[:size, :], 1, 0)).astype(bf16)
        back = dot(dgv, c[ti, :], 0, 0)
        if i > 0:
            db[: i * BLK, :] += back[: i * BLK]
        db[ti, :] = back[i * BLK :]


def final_kernel(
    heads, hg, place, own, other, msg, s_in, s_loc, th, x, b, dy, y, dxd, dbp, packed, skip,
    grad_x, db, grad_dt, d_cum,
):
    rows = x.shape[0]
    width = x.shape[1] // hg
    dt, _, _, w = head_columns(packed, heads, hg)
    xf = x[...].astype(f32)
    dyv = dy[...].astype(f32)
    dtl = lanes(dt, width)
    wl = lanes(w, width)
    core = place[0] % 2
    dsv = arriving(core, 1 - core, own, other, msg).astype(bf16)
    bds = dot(b[...], dsv, 1, 0)
    wx = (wl * dtl * xf).astype(bf16)
    db[...] = (dbp[...] + dot(wx, dsv, 1, 1)).astype(bf16)
    q = dxd[...] + wl * bds
    grad_x[...] = (dtl * q + skip[...] * dyv).astype(bf16)
    xd = (dtl * xf).astype(bf16).astype(f32)
    direct = xf * q
    cums = dyv * (y[...] - skip[...] * xf) - xd * dxd[...] - wx.astype(f32) * bds
    ends = dsv.astype(f32) * (
        th[...] * s_in[...].astype(f32) + s_loc[...].astype(f32)
    )
    last = lax.broadcasted_iota(jnp.int32, (rows, 1), 0) == rows - 1
    for h in range(hg):
        ls = slice(h * width, (h + 1) * width)
        grad_dt[0, :, h : h + 1] = jnp.sum(direct[:, ls], axis=1, keepdims=True)
        end = jnp.sum(jnp.sum(ends[:, ls], axis=0, keepdims=True), axis=1, keepdims=True)
        d_cum[0, :, h : h + 1] = jnp.sum(cums[:, ls], axis=1, keepdims=True) + jnp.where(
            last, end, 0.0
        )


def step_kernel(groups, raw, bias, decay, grad_dt, d_cum, out):
    rows, heads = raw.shape
    r = lax.broadcasted_iota(jnp.int32, (rows, rows), 0)
    c = lax.broadcasted_iota(jnp.int32, (rows, rows), 1)
    triu = (c >= r).astype(f32)
    direct = jnp.concatenate([grad_dt[g] for g in range(groups)], axis=1)
    dcv = jnp.concatenate([d_cum[g] for g in range(groups)], axis=1)
    de = dot(triu, dcv, 1, 0, lax.Precision.HIGHEST)
    v = raw[...] + bias[...]
    out[...] = (direct - decay[...] * de) / (1.0 + jnp.exp(-v))


def as_row(column):
    return jnp.transpose(jnp.broadcast_to(column, (column.shape[0], 128)))[0:1]


def as_column(row):
    return jnp.transpose(jnp.broadcast_to(row, (128, row.shape[1])))[:, 0:1]


def row_tail(row, width):
    row = jnp.concatenate([row, jnp.zeros((1, width - row.shape[1]), f32)], axis=1)
    return tail_of(row, bf16)


def project_kernel(mixed, w, head, before, out, along, token):
    rows = mixed.shape[0]
    value = dot(mixed[...], w[...], 1, 1)
    out[:rows, :] = value.astype(bf16)
    part = jnp.sum(value * head[...], axis=1, keepdims=True)
    along[...] = part + jnp.where(pl.program_id(0) == 0, before[...], along[...])
    if out.shape[0] > rows:
        out[rows:, :] = row_tail(as_row(along[...]), out.shape[1])
    token[...] = jnp.zeros_like(token)


def add_kernel(rows, a, b, out, token):
    out[:rows, :] = (a[:rows, :].astype(f32) + b[:rows, :].astype(f32)).astype(bf16)
    if rows < a.shape[0]:
        out[rows:, :] = tail_of(sum3(a[rows:, :]) + sum3(b[rows:, :]), bf16)
    token[...] = jnp.zeros_like(token)


def choose_kernel(rows, place, total, got, heads3, before, hidden, squares, token, *along):
    middle = (place[0] == 1) | (place[0] == 2)
    h = jnp.where(middle, total[:rows, :].astype(f32), got[:rows, :].astype(f32))
    if along:
        row = jnp.where(middle, sum3(total[rows:, :]), sum3(got[rows:, :]))
        along[0][...] = as_column(row[:, :rows])
    hidden[:rows, :] = h.astype(bf16)
    hidden[rows:, :] = heads3[...]
    squares[...] = before[...] + jnp.sum(h * h, axis=1, keepdims=True)
    token[...] = jnp.zeros_like(token)


def back_kernel(count, first, *refs):
    hiddens, weights, refs = refs[: count[0]], refs[count[0] : sum(count)], refs[sum(count) :]
    before, out, token = (None,) + refs if first else refs
    token[...] = jnp.zeros_like(token)
    value = None if first else before[...]
    at = 0
    for h in hiddens:
        for start in range(0, h.shape[1], weights[0].shape[0]):
            term = dot(h[:, start : start + weights[0].shape[0]], weights[at][...], 1, 0)
            value = term if value is None else value + term
            at += 1
    out[...] = value


def partner_kernel(off, pairs, out):
    rows, total = out.shape[0], pairs.shape[1]
    v = jnp.broadcast_to(pairs[...].astype(f32), (8, total))
    even = lax.broadcasted_iota(jnp.int32, (8, total), 1) % 2 == 0
    signed = jnp.where(even, -1.0 - pltpu.roll(v, total - 1, 1), 1.0 + pltpu.roll(v, 1, 1))
    tokens = (off[0] + lax.broadcasted_iota(jnp.int32, (rows, 1), 0)).astype(f32)
    acc = jnp.zeros((rows, 128), f32)
    for k in range(total // 128):
        ls = slice(k * 128, (k + 1) * 128)
        acc = acc + jnp.where(tokens == v[0:1, ls], signed[0:1, ls], 0.0)
    out[...] = jnp.sum(acc, axis=1, keepdims=True)


def vmem():
    return pl.BlockSpec(memory_space=pltpu.VMEM)


def smem():
    return pl.BlockSpec(memory_space=pltpu.SMEM)


def token_spec():
    return pl.BlockSpec((8, 128), lambda *at: (0, 0))


def call(
    kernel, grid, ins, outs, shapes, after=(), aliases=None, flops=0, size=0, limit=VMEM_LIMIT
):
    count = len(after)
    inner = (lambda *refs: kernel(*refs[count:])) if count else kernel
    run = pl.pallas_call(
        inner,
        grid=grid,
        in_specs=[pl.BlockSpec(memory_space=pl.ANY)] * count + list(ins),
        out_specs=outs,
        out_shape=shapes,
        input_output_aliases={k + count: v for k, v in (aliases or {}).items()},
        compiler_params=pltpu.CompilerParams(vmem_limit_bytes=limit),
        cost_estimate=pl.CostEstimate(flops=0, bytes_accessed=0, transcendentals=0),
    )
    return lambda *args: run(*after, *args)


def shape(dims, kind):
    return jax.ShapeDtypeStruct(dims, kind)


TOKEN = (8, 128)


def hops(count, distance):
    return [(i, i + distance) for i in range(count) if 0 <= i + distance < count]


def chain(message, forward, beside):
    count, place = lax.axis_size("seq"), lax.axis_index("seq").reshape(1)
    kind = message.dtype
    half = STATE // 2
    swap = [(i, i ^ 1) for i in range(count)]
    other = lax.ppermute(message, "seq", swap)
    pair_rows = half + message.shape[0] - STATE
    pair, pair_far, token = call(
        functools.partial(pair_kernel, forward),
        (),
        [smem(), vmem(), vmem()],
        [vmem(), vmem(), vmem()],
        [
            shape((pair_rows, message.shape[1]), kind),
            shape((half, message.shape[1]), bf16),
            shape(TOKEN, f32),
        ],
    )(place, message, other)
    way = 1 if forward else -1
    near = lax.ppermute(pair, "seq", hops(count, 2 * way))
    far = lax.ppermute(pair_far, "seq", hops(count, 4 * way))
    results, tokens = beside(token)
    own = call(
        enter_kernel,
        (),
        [vmem(), vmem()],
        vmem(),
        shape((half, message.shape[1]), kind),
        after=tokens,
    )(near, far)
    return own, lax.ppermute(own, "seq", swap), other, results


def pieces(count):
    unit = count // 8
    return [(unit * at, unit * size) for at, size in ((0, 1), (1, 2), (3, 2), (5, 2), (7, 1))]


def hidden_products(mixed, out_weight, reward_head):
    count, place = lax.axis_size("tensor"), lax.axis_index("tensor").reshape(1)
    rows, channels = mixed.shape
    model_width = out_weight.shape[0]
    plan = pieces(model_width)
    unit = model_width // 8
    line = count == 4
    tile = min(512, channels)
    column, column_spec = shape((rows, 1), f32), pl.BlockSpec((rows, 1), lambda j: (0, 0))
    head = reward_head[None, :]
    heads3 = jnp.concatenate(
        list(split3(head)) + [jnp.zeros((13, model_width), f32)], axis=0
    ).astype(bf16)

    def project(base, size, before, after, tail):
        step = size if tail else min(size, 256)
        return call(
            project_kernel,
            (size // step,),
            [
                pl.BlockSpec((rows, channels), lambda j: (0, 0)),
                pl.BlockSpec((step, channels), lambda j: (base // step + j, 0)),
                pl.BlockSpec((1, step), lambda j: (0, base // step + j)),
                column_spec,
            ],
            [
                pl.BlockSpec((rows + 16 * tail, step), lambda j: (0, j)),
                column_spec,
                token_spec(),
            ],
            [shape((rows + 16 * tail, size), bf16), column, shape(TOKEN, f32)],
            after=after,
            flops=2 * rows * channels * size,
            size=2 * channels * size,
            limit=STREAM_LIMIT,
        )(mixed, out_weight, head, before)

    def add(a, b, after):
        return call(
            functools.partial(add_kernel, rows),
            (),
            [vmem(), vmem()],
            [vmem(), vmem()],
            [shape(a.shape, bf16), shape(TOKEN, f32)],
            after=after,
            size=6 * a.size,
        )(a, b)

    def choose(k, total, got, squares, after):
        base, size = plan[k]
        tail = total.shape[0] > rows
        return call(
            functools.partial(choose_kernel, rows),
            (),
            [smem()] + [vmem()] * 4,
            [vmem()] * (3 + tail),
            [shape((rows + 16, size), bf16), column, shape(TOKEN, f32)] + [column] * tail,
            after=after,
            size=6 * total.size,
        )(place, total, got, heads3[:, base : base + size], squares)

    def back(hiddens, parts, before, after):
        first = before is None
        wide = pl.BlockSpec((rows + 16, tile), lambda j: (0, j))
        ins = [pl.BlockSpec((rows + 16, size), lambda j: (0, 0)) for _, size in parts]
        blocks = [base // unit + i for base, size in parts for i in range(size // unit)]
        ins += [pl.BlockSpec((unit, tile), lambda j, at=at: (at, j)) for at in blocks]
        total = unit * len(blocks)
        return call(
            functools.partial(back_kernel, (len(parts), len(blocks)), first),
            (channels // tile,),
            ins if first else ins + [wide],
            [wide, token_spec()],
            [shape((rows + 16, channels), f32), shape(TOKEN, f32)],
            after=after,
            aliases=None if first else {len(ins): 0},
            flops=2 * rows * channels * total,
            size=2 * channels * total + 8 * rows * channels,
            limit=STREAM_LIMIT,
        )(*hiddens, *[out_weight] * len(blocks), *(() if first else (before,)))

    squares = jnp.zeros((rows, 1), f32)
    along = jnp.zeros((rows, 1), f32)
    last = len(plan) - 1
    held = []
    if not line:
        for k, (base, size) in enumerate(plan):
            part, along, _ = project(base, size, along, (), False)
            h = lax.psum(part.astype(f32), "tensor").astype(bf16)
            squares = squares + jnp.sum(jnp.square(h.astype(f32)), axis=1, keepdims=True)
            h = jnp.concatenate([h, heads3[:, base : base + size]], axis=0)
            held.append(h)
        rest = lambda after: back(held[:-1], plan[:-1], None, after)[0]
        return rest, h, squares, lax.psum(along, "tensor")
    outward, across, inward = [(1, 0), (2, 3)], [(1, 2), (2, 1)], [(0, 1), (3, 2)]
    own, moved, sums, crossed, totals, got = {}, {}, {}, {}, {}, {}
    after = ()

    def start(k, along, after):
        own[k], along, token = project(*plan[k], along, after, k == last)
        moved[k] = lax.ppermute(own[k], "tensor", inward)
        return along, (token,)

    ahead = 2
    for k in range(ahead):
        along, after = start(k, along, after)
    for slot in range(len(plan) + 2):
        k = slot
        if k <= last:
            sums[k], token = add(own[k], moved[k], after)
            crossed[k] = lax.ppermute(sums[k], "tensor", across)
            after = (token,)
        if slot + ahead <= last:
            along, after = start(slot + ahead, along, after)
        k = slot - 1
        if 0 <= k <= last:
            totals[k], token = add(sums[k], crossed[k], after)
            got[k] = lax.ppermute(totals[k], "tensor", outward)
            after = (token,)
        if slot == last + 1:
            dm, token = back(held, plan[: len(held)], None, after)
            taken, after = len(held), (token,)
        k = slot - 2
        if 0 <= k <= last:
            h, squares, token, *column_out = choose(k, totals[k], got[k], squares, after)
            held.append(h)
            after = (token,)

    def rest(after):
        return back(held[taken:-1], plan[taken:-1], dm, after)[0]

    return rest, held[-1], squares, column_out[0]


def picked_rewards(rewards, partner, beside):
    rows = rewards.shape[0]
    count, place = lax.axis_size("seq"), lax.axis_index("seq")
    flat = rewards.reshape(rows)
    other = lax.ppermute(flat, "seq", [(i, i ^ 1) for i in range(count)])
    even = place % 2 == 0
    both = jnp.concatenate([jnp.where(even, flat, other), jnp.where(even, other, flat)])
    result = beside((both,))
    total = jnp.zeros((rows, 1), f32)
    for d in range(count // 2):
        seen = both
        if d:
            seen = lax.ppermute(both, "seq", [(i, i ^ (2 * d)) for i in range(count)])
        base = ((place // 2) ^ d) * 2 * rows
        at = (base + jnp.arange(2 * rows, dtype=jnp.int32)).astype(f32)
        total = total + jnp.sum(
            jnp.where(partner == at[None, :], seen[None, :], 0.0), axis=1, keepdims=True
        )
    return total, result


def on_device(
    ssd_input,
    gate_input,
    state_maps,
    step_raw,
    step_bias,
    decay_rate,
    skip_gain,
    norm_gain,
    out_weight,
    reward_head,
    traj_lengths,
    step_pairs,
):
    rows, channels = ssd_input.shape
    heads = step_raw.shape[1]
    width = channels // heads
    groups = state_maps.shape[2] // STATE
    hg = heads // groups
    gw = hg * width
    model_width = out_weight.shape[0]
    offset = lax.axis_index("seq") * rows
    maps = state_maps.reshape(rows, 2 * groups * STATE)
    bias2, decay2 = step_bias[None, :], decay_rate[None, :]
    skip = jnp.repeat(skip_gain, width)[None, :]
    gain = norm_gain[None, :]

    cols = pl.BlockSpec((rows, gw), lambda g: (0, g))
    row1 = pl.BlockSpec((1, gw), lambda g: (0, g))
    b_spec = pl.BlockSpec((rows, STATE), lambda g: (0, g))
    c_spec = pl.BlockSpec((rows, STATE), lambda g: (0, groups + g))
    state = pl.BlockSpec((STATE, gw), lambda g: (0, g))
    per_g = pl.BlockSpec((1, rows, hg), lambda g: (g, 0, 0))
    packed_spec = pl.BlockSpec((rows, 128), lambda g: (0, 0))
    per_gt = pl.BlockSpec((1, hg, rows), lambda g: (g, 0, 0))
    segc_spec = pl.BlockSpec((rows, 1), lambda g: (0, 0))
    segr_spec = pl.BlockSpec((8, rows), lambda g: (0, 0))
    grp = shape((groups, rows, hg), f32)

    packed, atg, dttg, segc, segr, s_msg = call(
        functools.partial(states_kernel, groups),
        (),
        [smem(), smem(), vmem(), vmem(), vmem(), vmem(), vmem()],
        [vmem()] * 6,
        [
            shape((rows, 128), f32),
            shape((groups, hg, rows), f32),
            shape((groups, hg, rows), f32),
            shape((rows, 1), f32),
            shape((8, rows), f32),
            shape((STATE + 16 if MSG == bf16 else STATE + 8, channels), MSG),
        ],
    )(offset.reshape(1), traj_lengths, step_raw, bias2, decay2, ssd_input, maps)

    place = lax.axis_index("seq").reshape(1)
    th = s_msg[STATE : STATE + 1]
    total = step_pairs.shape[0]

    def beside_forward(token):
        yw, t1 = call(
            functools.partial(within_kernel, heads),
            (groups,),
            [cols, b_spec, c_spec, per_gt, packed_spec, per_gt, segc_spec, segr_spec],
            [cols, token_spec()],
            [shape((rows, channels), f32), shape(TOKEN, f32)],
            after=(token,),
            flops=2 * rows * rows * channels,
            size=8 * rows * channels,
        )(ssd_input, maps, maps, dttg, packed, atg, segc, segr)
        found = call(
            partner_kernel,
            (),
            [smem(), vmem()],
            vmem(),
            shape((rows, 1), f32),
            after=(t1,),
        )(offset.reshape(1), step_pairs.reshape(1, total))
        return (yw, found), (found,)

    own_s, other_s, other_msg, (yw, found) = chain(s_msg, True, beside_forward)
    partner = jnp.abs(found) - 1.0
    side = jnp.where(found < 0, -1.0, 1.0)

    tail = s_msg.shape[0]
    half_spec = pl.BlockSpec((STATE // 2, gw), lambda g: (0, g))
    y, mixed, s_in = call(
        functools.partial(gate_kernel, heads, hg),
        (groups,),
        [
            smem(),
            cols,
            cols,
            cols,
            c_spec,
            packed_spec,
            half_spec,
            half_spec,
            pl.BlockSpec((tail, gw), lambda g: (0, g)),
            row1,
            row1,
        ],
        [cols, cols, state],
        [
            shape((rows, channels), f32),
            shape((rows, channels), bf16),
            shape((STATE, channels), bf16),
        ],
        flops=2 * rows * STATE * channels,
        size=14 * rows * channels,
    )(
        place,
        yw,
        ssd_input,
        gate_input,
        maps,
        packed,
        own_s,
        other_s,
        other_msg,
        skip,
        gain,
    )

    rest, hidden, squares, along = hidden_products(
        mixed, out_weight, reward_head
    )
    base, size = pieces(model_width)[-1]
    scale = jnp.sqrt(squares / model_width + norm_eps)
    rewards = along / scale
    picked, dm = picked_rewards(rewards, partner, rest)
    push = loss_scale * jax.nn.sigmoid(side * (rewards - picked))
    own_grad = side * push
    p1 = own_grad / scale
    p2 = own_grad * along / (model_width * scale * scale * scale)

    grad_gate, dy, g_state = call(
        functools.partial(gate_back_kernel, heads, hg),
        (groups,),
        [
            pl.BlockSpec((rows + 16, gw), lambda g: (0, g)),
            pl.BlockSpec((rows + 16, size), lambda g: (0, 0)),
            pl.BlockSpec((size, gw), lambda g: (base // size, g)),
            segc_spec,
            segc_spec,
            cols,
            cols,
            row1,
            c_spec,
            packed_spec,
            row1,
        ],
        [cols, cols, pl.BlockSpec((STATE + 16, gw), lambda g: (0, g))],
        [
            shape((rows, channels), bf16),
            shape((rows, channels), bf16),
            shape((STATE + 16, channels), bf16),
        ],
        flops=2 * rows * STATE * channels,
        size=14 * rows * channels,
        limit=STREAM_LIMIT,
    )(dm, hidden, out_weight, p1, p2, y, gate_input, gain, maps, packed, th)

    def beside_back(token):
        dxd, dc, dbp, t1 = call(
            functools.partial(within_back_kernel, heads),
            (groups,),
            [
                cols,
                b_spec,
                c_spec,
                packed_spec,
                per_gt,
                segc_spec,
                segr_spec,
                cols,
                state,
            ],
            [cols, b_spec, b_spec, token_spec()],
            [
                shape((rows, channels), f32),
                shape((rows, groups * STATE), bf16),
                shape((rows, groups * STATE), f32),
                shape(TOKEN, f32),
            ],
            after=(token,),
            flops=4 * rows * rows * channels,
            size=10 * rows * channels,
        )(ssd_input, maps, maps, packed, atg, segc, segr, dy, s_in)
        return (dxd, dc, dbp), (t1,)

    own_d, other_d, other_g, (dxd, dc, dbp) = chain(g_state, False, beside_back)

    grad_input, db, grad_dt, d_cum = call(
        functools.partial(final_kernel, heads, hg),
        (groups,),
        [
            smem(),
            half_spec,
            half_spec,
            pl.BlockSpec((STATE + 16, gw), lambda g: (0, g)),
            state,
            state,
            row1,
            cols,
            b_spec,
            cols,
            cols,
            cols,
            b_spec,
            packed_spec,
            row1,
        ],
        [cols, b_spec, per_g, per_g],
        [
            shape((rows, channels), bf16),
            shape((rows, groups * STATE), bf16),
            grp,
            grp,
        ],
        flops=4 * rows * STATE * channels,
        size=16 * rows * channels,
    )(
        place,
        own_d,
        other_d,
        other_g,
        s_in,
        s_msg,
        th,
        ssd_input,
        maps,
        dy,
        y,
        dxd,
        dbp,
        packed,
        skip,
    )
    grad_step = call(
        functools.partial(step_kernel, groups),
        (),
        [vmem()] * 5,
        vmem(),
        shape((rows, heads), f32),
    )(step_raw, bias2, decay2, grad_dt, d_cum)
    grad_maps = jnp.stack([db, dc], axis=1)
    return (rewards.reshape(rows), grad_input, grad_gate, grad_maps, grad_step)


def solution(mesh):
    return jax.shard_map(
        on_device,
        mesh=mesh,
        in_specs=(
            P("seq", "tensor"),
            P("seq", "tensor"),
            P("seq", None, "tensor"),
            P("seq", "tensor"),
            P("tensor"),
            P("tensor"),
            P("tensor"),
            P("tensor"),
            P(None, "tensor"),
            P(),
            P(),
            P(),
        ),
        out_specs=(
            P("seq"),
            P("seq", "tensor"),
            P("seq", "tensor"),
            P("seq", None, "tensor"),
            P("seq", "tensor"),
        ),
        check_vma=False,
    )
```

```python
import functools

import jax
import jax.numpy as jnp
from jax import lax
from jax.experimental import pallas as pl
from jax.experimental.pallas import tpu as pltpu
from jax.sharding import PartitionSpec as P

STATE = 128
BLK = 128
norm_eps = 1e-05
loss_scale = 64.0
f32 = jnp.float32
bf16 = jnp.bfloat16
VMEM_LIMIT = 24 * 1024 * 1024
STREAM_LIMIT = 49 * 1024 * 1024


def dot(a, b, ca, cb, precision=None):
    return lax.dot_general(
        a, b, (((ca,), (cb,)), ((), ())), precision=precision, preferred_element_type=f32
    )


MSG = f32


def dot_hi_lo(a, b, ca, cb):
    hi = a.astype(bf16)
    lo = (a - hi.astype(f32)).astype(bf16)
    return dot(hi, b, ca, cb) + dot(lo, b, ca, cb)


def rounded(v):
    return lax.reduce_precision(v, exponent_bits=8, mantissa_bits=7)


def split3(v):
    hi = rounded(v)
    mid = rounded(v - hi)
    lo = rounded(v - hi - mid)
    return hi, mid, lo


def split3_in(v):
    hi = v.astype(bf16).astype(f32)
    mid = (v - hi).astype(bf16).astype(f32)
    lo = (v - hi - mid).astype(bf16).astype(f32)
    return hi, mid, lo


def lanes(cols, width):
    rows = cols.shape[0]
    return jnp.concatenate(
        [jnp.broadcast_to(cols[:, h : h + 1], (rows, width)) for h in range(cols.shape[1])], axis=1
    )


def states_kernel(
    groups, off, lens, raw, bias, decay, x, maps, packed, atg, dttg, segc, segr, s_msg
):
    rows, heads = raw.shape
    hg = heads // groups
    width = x.shape[1] // heads
    v = raw[...] + bias[...]
    dt = jnp.maximum(v, 0.0) + jnp.log1p(jnp.exp(-jnp.abs(v)))
    e = -dt * decay[...]
    r = lax.broadcasted_iota(jnp.int32, (rows, rows), 0)
    c = lax.broadcasted_iota(jnp.int32, (rows, rows), 1)
    tril = (c <= r).astype(f32)
    cum = dot(tril, e, 1, 0, lax.Precision.HIGHEST)
    cum_t = dot(e, tril, 0, 1, lax.Precision.HIGHEST)
    eye = (c == r).astype(f32)
    dt_t = dot(dt, eye, 0, 0, lax.Precision.HIGHEST)
    pos = off[0] + lax.broadcasted_iota(jnp.int32, (rows, 128), 0)
    opening = jnp.int32(0)
    starts = jnp.zeros((rows, 128), f32)
    for k in range(lens.shape[0]):
        starts = jnp.where(pos == opening, 1.0, starts)
        opening = opening + lens[k]
    seg = dot(tril, starts, 1, 0)[:, :1]
    segc[...] = seg
    segr[...] = dot(starts, tril, 0, 1)[:8]
    seg_last = seg[rows - 1 : rows]
    last = cum[rows - 1 : rows]
    w = jnp.where(seg == seg_last, jnp.exp(last - cum), 0.0)
    f = jnp.where(seg == 0.0, jnp.exp(cum), 0.0)
    th = jnp.where(seg_last == 0.0, jnp.exp(last), 0.0)
    wdt = w * dt
    fill = jnp.zeros((rows, 128 - 4 * heads), f32)
    packed[...] = jnp.concatenate([dt, cum, f, w, fill], axis=1)
    for g in range(groups):
        hs = slice(g * hg, (g + 1) * hg)
        ls = slice(g * hg * width, (g + 1) * hg * width)
        atg[g] = cum_t[hs]
        dttg[g] = dt_t[hs]
        wx = lanes(wdt[:, hs], width) * x[:, ls].astype(f32)
        b_rows = maps[:, g * STATE : (g + 1) * STATE]
        wx_hi = wx.astype(bf16)
        wx_lo = (wx - wx_hi.astype(f32)).astype(bf16)
        s_msg[0:STATE, ls] = (dot(b_rows, wx_hi, 0, 0) + dot(b_rows, wx_lo, 0, 0)).astype(s_msg.dtype)
        if s_msg.dtype == f32:
            s_msg[STATE : STATE + 8, ls] = jnp.broadcast_to(
                lanes(th[:, hs], width), (8, hg * width)
            )
            continue
        hi, mid, lo = split3_in(lanes(th[:, hs], width))
        row = lax.broadcasted_iota(jnp.int32, (16, hg * width), 0)
        tail = jnp.where(row == 0, hi, jnp.where(row == 1, mid, jnp.where(row == 2, lo, 0.0)))
        s_msg[STATE : STATE + 16, ls] = tail.astype(bf16)


def head_columns(packed, heads, count):
    shift = (128 - count * pl.program_id(0)) % 128
    turned = pltpu.roll(packed[...], shift, 1)
    return [turned[:, k * heads : k * heads + count] for k in range(4)]


def mask_terms(segc, segr, i):
    size = (i + 1) * BLK
    r = i * BLK + lax.broadcasted_iota(jnp.int32, (BLK, size), 0)
    c = lax.broadcasted_iota(jnp.int32, (BLK, size), 1)
    ok = (c <= r) & (segc[i * BLK : (i + 1) * BLK, :] == segr[0:1, :size])
    return jnp.where(ok, 0.0, -1e30)


def within_kernel(heads, x, b, c, dtt, packed, atg, segc, segr, yw, token):
    token[...] = jnp.zeros_like(token)
    rows = x.shape[0]
    hg = atg.shape[1]
    _, cum, _, _ = head_columns(packed, heads, hg)
    width = x.shape[1] // hg
    for i in range(rows // BLK):
        ti, size = slice(i * BLK, (i + 1) * BLK), (i + 1) * BLK
        scores = dot(c[ti, :], b[:size, :], 1, 1)
        neg = mask_terms(segc, segr, i)
        for h in range(hg):
            decays = jnp.exp(cum[ti, h : h + 1] - atg[0, h : h + 1, :size] + neg)
            m = decays * scores * dtt[0, h : h + 1, :size]
            yw[ti, h * width : (h + 1) * width] = dot_hi_lo(
                m, x[:size, h * width : (h + 1) * width], 1, 0
            )


def sum3(rows):
    rows = rows.astype(f32)
    return (rows[0:1] + rows[1:2]) + rows[2:3]


def through_of(rows):
    if rows.dtype == f32:
        return rows[0:1]
    return sum3(rows)


def tail_of(through, kind):
    if kind == f32:
        return jnp.broadcast_to(through, (8, through.shape[1]))
    hi, mid, lo = split3_in(through)
    row = lax.broadcasted_iota(jnp.int32, (16, through.shape[1]), 0)
    tail = jnp.where(row == 0, hi, jnp.where(row == 1, mid, jnp.where(row == 2, lo, 0.0)))
    return tail.astype(bf16)


def pair_kernel(forward, place, message, other, out, far, token):
    core = place[0] % 2
    half = STATE // 2
    late = core if forward else 1 - core
    start = pl.multiple_of(core * half, half)
    mine, theirs = message[pl.ds(start, half), :], other[pl.ds(start, half), :]
    mine, theirs = mine.astype(f32), theirs.astype(f32)
    th_mine, th_theirs = through_of(message[STATE:, :]), through_of(other[STATE:, :])
    is_late = late == 1
    pair = jnp.where(is_late, mine + th_mine * theirs, theirs + th_theirs * mine)
    out[0:half, :] = pair.astype(out.dtype)
    out[half:, :] = tail_of(th_mine * th_theirs, out.dtype)
    far[...] = pair.astype(bf16)
    token[...] = jnp.zeros_like(token)


def enter_kernel(near, far, out):
    half = STATE // 2
    out[...] = (
        near[0:half, :].astype(f32) + through_of(near[half:, :]) * far[...].astype(f32)
    ).astype(out.dtype)


def arriving(core, late, own, other, msg):
    half = STATE // 2
    mine, theirs = own[...].astype(f32), other[...].astype(f32)
    low = jnp.where(core == 0, mine, theirs)
    high = jnp.where(core == 0, theirs, mine)
    whole = jnp.concatenate([low, high], axis=0)
    passed = msg[0:STATE, :].astype(f32) + through_of(msg[STATE:, :]) * whole
    return jnp.where(late == 1, passed, whole)


def gate_kernel(
    heads, hg, place, yw, x, z, c, packed, own, other, msg, skip, gain, y, mixed, s_in
):
    width = x.shape[1] // hg
    _, _, f, _ = head_columns(packed, heads, hg)
    state = arriving(place[0] % 2, place[0] % 2, own, other, msg)
    s_hi = state.astype(bf16)
    s_lo = (state - s_hi.astype(f32)).astype(bf16)
    s_in[...] = s_hi
    out = (
        yw[...]
        + lanes(f, width) * (dot(c[...], s_hi, 1, 0) + dot(c[...], s_lo, 1, 0))
        + skip[...] * x[...].astype(f32)
    )
    y[...] = out
    zf = z[...].astype(f32)
    gated = out * zf / (1.0 + jnp.exp(-zf))
    mean = jnp.mean(gated * gated, axis=1, keepdims=True)
    mixed[...] = (gated * lax.rsqrt(mean + norm_eps) * gain[...]).astype(bf16)


def add_products(value, hiddens, weights):
    at = 0
    for h in hiddens:
        for start in range(0, h.shape[1], weights[0].shape[0]):
            term = dot(h[:, start : start + weights[0].shape[0]], weights[at][...], 1, 0)
            value = term if value is None else value + term
            at += 1
    return value


def gate_back_kernel(
    heads, hg, count, dm, *refs
):
    hiddens, weights = refs[: count[0]], refs[count[0] : sum(count)]
    p1, p2, y, z, gain, c, packed, th, grad_z, dy, g_state = refs[sum(count) :]
    rows = z.shape[0]
    width = z.shape[1] // hg
    _, _, f, _ = head_columns(packed, heads, hg)
    products = add_products(dm[...], hiddens, weights)
    d_mixed = p1[...] * sum3(products[rows:]) - p2[...] * products[:rows]
    zf = z[...].astype(f32)
    sig = 1.0 / (1.0 + jnp.exp(-zf))
    silu = zf * sig
    yv = y[...]
    gated = yv * silu
    inv = lax.rsqrt(jnp.mean(gated * gated, axis=1, keepdims=True) + norm_eps)
    dn = d_mixed * gain[...]
    corr = jnp.mean(dn * gated, axis=1, keepdims=True)
    dgated = inv * dn - gated * (inv * inv * inv * corr)
    grad_z[...] = (dgated * yv * (sig * (1.0 + zf * (1.0 - sig)))).astype(bf16)
    dyv = (dgated * silu).astype(bf16)
    dy[...] = dyv
    fdy = (lanes(f, width) * dyv.astype(f32)).astype(bf16)
    g_state[0:STATE, :] = dot(c[...], fdy, 0, 0).astype(bf16)
    g_state[STATE:, :] = tail_of(th[...], bf16)


def within_back_kernel(
    heads, x, b, c, packed, atg, segc, segr, dy, s_in, dxd, dc, db, token
):
    rows = x.shape[0]
    hg = atg.shape[1]
    width = x.shape[1] // hg
    dt, cum, f, _ = head_columns(packed, heads, hg)
    xd = (lanes(dt, width) * x[...].astype(f32)).astype(bf16)
    dyv = dy[...]
    fdy = (lanes(f, width) * dyv.astype(f32)).astype(bf16)
    token[...] = jnp.zeros_like(token)
    carried = dot(fdy, s_in[...], 1, 1)
    for i in range(rows // BLK):
        ti, size = slice(i * BLK, (i + 1) * BLK), (i + 1) * BLK
        scores = dot(c[ti, :], b[:size, :], 1, 1)
        neg = mask_terms(segc, segr, i)
        total = jnp.zeros((BLK, size), f32)
        for h in range(hg):
            ls = slice(h * width, (h + 1) * width)
            decays = jnp.exp(cum[ti, h : h + 1] - atg[0, h : h + 1, :size] + neg)
            m = (decays * scores).astype(bf16)
            total = total + decays * dot(dyv[ti, ls], xd[:size, ls], 1, 1)
            back = dot(m, dyv[ti, ls], 0, 0)
            if i > 0:
                dxd[: i * BLK, ls] += back[: i * BLK]
            dxd[ti, ls] = back[i * BLK :]
        dgv = total.astype(bf16)
        dc[ti, :] = (carried[ti] + dot(dgv, b[:size, :], 1, 0)).astype(bf16)
        back = dot(dgv, c[ti, :], 0, 0)
        if i > 0:
            db[: i * BLK, :] += back[: i * BLK]
        db[ti, :] = back[i * BLK :]


def final_kernel(
    heads, hg, place, own, other, msg, s_in, s_loc, th, x, b, dy, y, dxd, dbp, packed, skip,
    grad_x, db, grad_dt, d_cum,
):
    rows = x.shape[0]
    width = x.shape[1] // hg
    dt, _, _, w = head_columns(packed, heads, hg)
    xf = x[...].astype(f32)
    dyv = dy[...].astype(f32)
    dtl = lanes(dt, width)
    wl = lanes(w, width)
    core = place[0] % 2
    dsv = arriving(core, 1 - core, own, other, msg).astype(bf16)
    bds = dot(b[...], dsv, 1, 0)
    wx = (wl * dtl * xf).astype(bf16)
    db[...] = (dbp[...] + dot(wx, dsv, 1, 1)).astype(bf16)
    q = dxd[...] + wl * bds
    grad_x[...] = (dtl * q + skip[...] * dyv).astype(bf16)
    xd = (dtl * xf).astype(bf16).astype(f32)
    direct = xf * q
    cums = dyv * (y[...] - skip[...] * xf) - xd * dxd[...] - wx.astype(f32) * bds
    ends = dsv.astype(f32) * (
        th[...] * s_in[...].astype(f32) + s_loc[...].astype(f32)
    )
    last = lax.broadcasted_iota(jnp.int32, (rows, 1), 0) == rows - 1
    for h in range(hg):
        ls = slice(h * width, (h + 1) * width)
        grad_dt[0, :, h : h + 1] = jnp.sum(direct[:, ls], axis=1, keepdims=True)
        end = jnp.sum(jnp.sum(ends[:, ls], axis=0, keepdims=True), axis=1, keepdims=True)
        d_cum[0, :, h : h + 1] = jnp.sum(cums[:, ls], axis=1, keepdims=True) + jnp.where(
            last, end, 0.0
        )


def step_kernel(groups, raw, bias, decay, grad_dt, d_cum, out):
    rows, heads = raw.shape
    r = lax.broadcasted_iota(jnp.int32, (rows, rows), 0)
    c = lax.broadcasted_iota(jnp.int32, (rows, rows), 1)
    triu = (c >= r).astype(f32)
    direct = jnp.concatenate([grad_dt[g] for g in range(groups)], axis=1)
    dcv = jnp.concatenate([d_cum[g] for g in range(groups)], axis=1)
    de = dot(triu, dcv, 1, 0, lax.Precision.HIGHEST)
    v = raw[...] + bias[...]
    out[...] = (direct - decay[...] * de) / (1.0 + jnp.exp(-v))


def as_row(column):
    return jnp.transpose(jnp.broadcast_to(column, (column.shape[0], 128)))[0:1]


def as_column(row):
    return jnp.transpose(jnp.broadcast_to(row, (128, row.shape[1])))[:, 0:1]


def row_tail(row, width):
    row = jnp.concatenate([row, jnp.zeros((1, width - row.shape[1]), f32)], axis=1)
    return tail_of(row, bf16)


def project_kernel(mixed, w, head, before, out, along, token):
    rows = mixed.shape[0]
    value = dot(mixed[...], w[...], 1, 1)
    out[:rows, :] = value.astype(bf16)
    part = jnp.sum(value * head[...], axis=1, keepdims=True)
    along[...] = part + jnp.where(pl.program_id(0) == 0, before[...], along[...])
    if out.shape[0] > rows:
        out[rows:, :] = row_tail(as_row(along[...]), out.shape[1])
    token[...] = jnp.zeros_like(token)


def add_kernel(rows, a, b, out, token):
    out[:rows, :] = (a[:rows, :].astype(f32) + b[:rows, :].astype(f32)).astype(bf16)
    if rows < a.shape[0]:
        out[rows:, :] = tail_of(sum3(a[rows:, :]) + sum3(b[rows:, :]), bf16)
    token[...] = jnp.zeros_like(token)


def choose_kernel(rows, place, total, got, heads3, before, hidden, squares, token, *along):
    middle = (place[0] == 1) | (place[0] == 2)
    h = jnp.where(middle, total[:rows, :].astype(f32), got[:rows, :].astype(f32))
    if along:
        row = jnp.where(middle, sum3(total[rows:, :]), sum3(got[rows:, :]))
        along[0][...] = as_column(row[:, :rows])
    hidden[:rows, :] = h.astype(bf16)
    hidden[rows:, :] = heads3[...]
    squares[...] = before[...] + jnp.sum(h * h, axis=1, keepdims=True)
    token[...] = jnp.zeros_like(token)


def back_kernel(count, first, *refs):
    hiddens, weights, refs = refs[: count[0]], refs[count[0] : sum(count)], refs[sum(count) :]
    before, out, token = (None,) + refs if first else refs
    token[...] = jnp.zeros_like(token)
    out[...] = add_products(None if first else before[...], hiddens, weights)


def partner_kernel(off, pairs, out):
    rows, total = out.shape[0], pairs.shape[1]
    v = jnp.broadcast_to(pairs[...].astype(f32), (8, total))
    even = lax.broadcasted_iota(jnp.int32, (8, total), 1) % 2 == 0
    signed = jnp.where(even, -1.0 - pltpu.roll(v, total - 1, 1), 1.0 + pltpu.roll(v, 1, 1))
    tokens = (off[0] + lax.broadcasted_iota(jnp.int32, (rows, 1), 0)).astype(f32)
    acc = jnp.zeros((rows, 128), f32)
    for k in range(total // 128):
        ls = slice(k * 128, (k + 1) * 128)
        acc = acc + jnp.where(tokens == v[0:1, ls], signed[0:1, ls], 0.0)
    out[...] = jnp.sum(acc, axis=1, keepdims=True)


def vmem():
    return pl.BlockSpec(memory_space=pltpu.VMEM)


def smem():
    return pl.BlockSpec(memory_space=pltpu.SMEM)


def token_spec():
    return pl.BlockSpec((8, 128), lambda *at: (0, 0))


def call(
    kernel, grid, ins, outs, shapes, after=(), aliases=None, flops=0, size=0, limit=VMEM_LIMIT
):
    count = len(after)
    inner = (lambda *refs: kernel(*refs[count:])) if count else kernel
    run = pl.pallas_call(
        inner,
        grid=grid,
        in_specs=[pl.BlockSpec(memory_space=pl.ANY)] * count + list(ins),
        out_specs=outs,
        out_shape=shapes,
        input_output_aliases={k + count: v for k, v in (aliases or {}).items()},
        compiler_params=pltpu.CompilerParams(vmem_limit_bytes=limit),
        cost_estimate=pl.CostEstimate(flops=flops // 4, bytes_accessed=size // 4, transcendentals=0),
    )
    return lambda *args: run(*after, *args)


def shape(dims, kind):
    return jax.ShapeDtypeStruct(dims, kind)


TOKEN = (8, 128)


def hops(count, distance):
    return [(i, i + distance) for i in range(count) if 0 <= i + distance < count]


def chain(message, forward, beside):
    count, place = lax.axis_size("seq"), lax.axis_index("seq").reshape(1)
    kind = message.dtype
    half = STATE // 2
    swap = [(i, i ^ 1) for i in range(count)]
    other = lax.ppermute(message, "seq", swap)
    pair_rows = half + message.shape[0] - STATE
    pair, pair_far, token = call(
        functools.partial(pair_kernel, forward),
        (),
        [smem(), vmem(), vmem()],
        [vmem(), vmem(), vmem()],
        [
            shape((pair_rows, message.shape[1]), kind),
            shape((half, message.shape[1]), bf16),
            shape(TOKEN, f32),
        ],
    )(place, message, other)
    way = 1 if forward else -1
    near = lax.ppermute(pair, "seq", hops(count, 2 * way))
    far = lax.ppermute(pair_far, "seq", hops(count, 4 * way))
    results, tokens = beside(token)
    own = call(
        enter_kernel,
        (),
        [vmem(), vmem()],
        vmem(),
        shape((half, message.shape[1]), kind),
        after=tokens,
    )(near, far)
    return own, lax.ppermute(own, "seq", swap), other, results


def pieces(count):
    unit = count // 8
    return [(unit * at, unit * size) for at, size in ((0, 1), (1, 2), (3, 2), (5, 2), (7, 1))]


def hidden_products(mixed, out_weight, reward_head):
    count, place = lax.axis_size("tensor"), lax.axis_index("tensor").reshape(1)
    rows, channels = mixed.shape
    model_width = out_weight.shape[0]
    plan = pieces(model_width)
    unit = model_width // 8
    line = count == 4
    tile = min(512, channels)
    column, column_spec = shape((rows, 1), f32), pl.BlockSpec((rows, 1), lambda j: (0, 0))
    head = reward_head[None, :]
    heads3 = jnp.concatenate(
        list(split3(head)) + [jnp.zeros((13, model_width), f32)], axis=0
    ).astype(bf16)

    def project(base, size, before, after, tail):
        step = size if tail else min(size, 256)
        return call(
            project_kernel,
            (size // step,),
            [
                pl.BlockSpec((rows, channels), lambda j: (0, 0)),
                pl.BlockSpec((step, channels), lambda j: (base // step + j, 0)),
                pl.BlockSpec((1, step), lambda j: (0, base // step + j)),
                column_spec,
            ],
            [
                pl.BlockSpec((rows + 16 * tail, step), lambda j: (0, j)),
                column_spec,
                token_spec(),
            ],
            [shape((rows + 16 * tail, size), bf16), column, shape(TOKEN, f32)],
            after=after,
            flops=2 * rows * channels * size,
            size=2 * channels * size,
            limit=STREAM_LIMIT,
        )(mixed, out_weight, head, before)

    def add(a, b, after):
        return call(
            functools.partial(add_kernel, rows),
            (),
            [vmem(), vmem()],
            [vmem(), vmem()],
            [shape(a.shape, bf16), shape(TOKEN, f32)],
            after=after,
            size=6 * a.size,
        )(a, b)

    def choose(k, total, got, squares, after):
        base, size = plan[k]
        tail = total.shape[0] > rows
        return call(
            functools.partial(choose_kernel, rows),
            (),
            [smem()] + [vmem()] * 4,
            [vmem()] * (3 + tail),
            [shape((rows + 16, size), bf16), column, shape(TOKEN, f32)] + [column] * tail,
            after=after,
            size=6 * total.size,
        )(place, total, got, heads3[:, base : base + size], squares)

    def back(hiddens, parts, before, after):
        first = before is None
        wide = pl.BlockSpec((rows + 16, tile), lambda j: (0, j))
        ins = [pl.BlockSpec((rows + 16, size), lambda j: (0, 0)) for _, size in parts]
        blocks = [base // unit + i for base, size in parts for i in range(size // unit)]
        ins += [pl.BlockSpec((unit, tile), lambda j, at=at: (at, j)) for at in blocks]
        total = unit * len(blocks)
        return call(
            functools.partial(back_kernel, (len(parts), len(blocks)), first),
            (channels // tile,),
            ins if first else ins + [wide],
            [wide, token_spec()],
            [shape((rows + 16, channels), f32), shape(TOKEN, f32)],
            after=after,
            aliases=None if first else {len(ins): 0},
            flops=2 * rows * channels * total,
            size=2 * channels * total + 8 * rows * channels,
            limit=STREAM_LIMIT,
        )(*hiddens, *[out_weight] * len(blocks), *(() if first else (before,)))

    squares = jnp.zeros((rows, 1), f32)
    along = jnp.zeros((rows, 1), f32)
    last = len(plan) - 1
    held = []
    if not line:
        for k, (base, size) in enumerate(plan):
            part, along, _ = project(base, size, along, (), False)
            h = lax.psum(part.astype(f32), "tensor").astype(bf16)
            squares = squares + jnp.sum(jnp.square(h.astype(f32)), axis=1, keepdims=True)
            h = jnp.concatenate([h, heads3[:, base : base + size]], axis=0)
            held.append(h)
        dm, _ = back(held[:-2], plan[:-2], None, ())
        return dm, held[-2:], squares, lax.psum(along, "tensor")
    outward, across, inward = [(1, 0), (2, 3)], [(1, 2), (2, 1)], [(0, 1), (3, 2)]
    own, moved, sums, crossed, totals, got = {}, {}, {}, {}, {}, {}
    after = ()

    def start(k, along, after):
        own[k], along, token = project(*plan[k], along, after, k == last)
        moved[k] = lax.ppermute(own[k], "tensor", inward)
        return along, (token,)

    ahead = 2
    for k in range(ahead):
        along, after = start(k, along, after)
    for slot in range(len(plan) + 2):
        k = slot
        if k <= last:
            sums[k], token = add(own[k], moved[k], after)
            crossed[k] = lax.ppermute(sums[k], "tensor", across)
            after = (token,)
        if slot + ahead <= last:
            along, after = start(slot + ahead, along, after)
        k = slot - 1
        if 0 <= k <= last:
            totals[k], token = add(sums[k], crossed[k], after)
            got[k] = lax.ppermute(totals[k], "tensor", outward)
            after = (token,)
        if slot == last + 1:
            dm, token = back(held, plan[: len(held)], None, after)
            after = (token,)
        k = slot - 2
        if 0 <= k <= last:
            h, squares, token, *column_out = choose(k, totals[k], got[k], squares, after)
            held.append(h)
            after = (token,)

    return dm, held[-2:], squares, column_out[0]


def picked_rewards(rewards, partner):
    rows = rewards.shape[0]
    count, place = lax.axis_size("seq"), lax.axis_index("seq")
    flat = rewards.reshape(rows)
    other = lax.ppermute(flat, "seq", [(i, i ^ 1) for i in range(count)])
    even = place % 2 == 0
    both = jnp.concatenate([jnp.where(even, flat, other), jnp.where(even, other, flat)])
    total = jnp.zeros((rows, 1), f32)
    for d in range(count // 2):
        seen = both
        if d:
            seen = lax.ppermute(both, "seq", [(i, i ^ (2 * d)) for i in range(count)])
        base = ((place // 2) ^ d) * 2 * rows
        at = (base + jnp.arange(2 * rows, dtype=jnp.int32)).astype(f32)
        total = total + jnp.sum(
            jnp.where(partner == at[None, :], seen[None, :], 0.0), axis=1, keepdims=True
        )
    return total


def on_device(
    ssd_input,
    gate_input,
    state_maps,
    step_raw,
    step_bias,
    decay_rate,
    skip_gain,
    norm_gain,
    out_weight,
    reward_head,
    traj_lengths,
    step_pairs,
):
    rows, channels = ssd_input.shape
    heads = step_raw.shape[1]
    width = channels // heads
    groups = state_maps.shape[2] // STATE
    hg = heads // groups
    gw = hg * width
    model_width = out_weight.shape[0]
    offset = lax.axis_index("seq") * rows
    maps = state_maps.reshape(rows, 2 * groups * STATE)
    bias2, decay2 = step_bias[None, :], decay_rate[None, :]
    skip = jnp.repeat(skip_gain, width)[None, :]
    gain = norm_gain[None, :]

    cols = pl.BlockSpec((rows, gw), lambda g: (0, g))
    row1 = pl.BlockSpec((1, gw), lambda g: (0, g))
    b_spec = pl.BlockSpec((rows, STATE), lambda g: (0, g))
    c_spec = pl.BlockSpec((rows, STATE), lambda g: (0, groups + g))
    state = pl.BlockSpec((STATE, gw), lambda g: (0, g))
    per_g = pl.BlockSpec((1, rows, hg), lambda g: (g, 0, 0))
    packed_spec = pl.BlockSpec((rows, 128), lambda g: (0, 0))
    per_gt = pl.BlockSpec((1, hg, rows), lambda g: (g, 0, 0))
    segc_spec = pl.BlockSpec((rows, 1), lambda g: (0, 0))
    segr_spec = pl.BlockSpec((8, rows), lambda g: (0, 0))
    grp = shape((groups, rows, hg), f32)

    packed, atg, dttg, segc, segr, s_msg = call(
        functools.partial(states_kernel, groups),
        (),
        [smem(), smem(), vmem(), vmem(), vmem(), vmem(), vmem()],
        [vmem()] * 6,
        [
            shape((rows, 128), f32),
            shape((groups, hg, rows), f32),
            shape((groups, hg, rows), f32),
            shape((rows, 1), f32),
            shape((8, rows), f32),
            shape((STATE + 16 if MSG == bf16 else STATE + 8, channels), MSG),
        ],
    )(offset.reshape(1), traj_lengths, step_raw, bias2, decay2, ssd_input, maps)

    place = lax.axis_index("seq").reshape(1)
    th = s_msg[STATE : STATE + 1]
    total = step_pairs.shape[0]

    def beside_forward(token):
        yw, t1 = call(
            functools.partial(within_kernel, heads),
            (groups,),
            [cols, b_spec, c_spec, per_gt, packed_spec, per_gt, segc_spec, segr_spec],
            [cols, token_spec()],
            [shape((rows, channels), f32), shape(TOKEN, f32)],
            after=(token,),
            flops=2 * rows * rows * channels,
            size=8 * rows * channels,
        )(ssd_input, maps, maps, dttg, packed, atg, segc, segr)
        found = call(
            partner_kernel,
            (),
            [smem(), vmem()],
            vmem(),
            shape((rows, 1), f32),
            after=(t1,),
        )(offset.reshape(1), step_pairs.reshape(1, total))
        return (yw, found), (found,)

    own_s, other_s, other_msg, (yw, found) = chain(s_msg, True, beside_forward)
    partner = jnp.abs(found) - 1.0
    side = jnp.where(found < 0, -1.0, 1.0)

    tail = s_msg.shape[0]
    half_spec = pl.BlockSpec((STATE // 2, gw), lambda g: (0, g))
    y, mixed, s_in = call(
        functools.partial(gate_kernel, heads, hg),
        (groups,),
        [
            smem(),
            cols,
            cols,
            cols,
            c_spec,
            packed_spec,
            half_spec,
            half_spec,
            pl.BlockSpec((tail, gw), lambda g: (0, g)),
            row1,
            row1,
        ],
        [cols, cols, state],
        [
            shape((rows, channels), f32),
            shape((rows, channels), bf16),
            shape((STATE, channels), bf16),
        ],
        flops=2 * rows * STATE * channels,
        size=14 * rows * channels,
    )(
        place,
        yw,
        ssd_input,
        gate_input,
        maps,
        packed,
        own_s,
        other_s,
        other_msg,
        skip,
        gain,
    )

    dm, hidden, squares, along = hidden_products(
        mixed, out_weight, reward_head
    )
    unit = model_width // 8
    late = pieces(model_width)[-2:]
    blocks = [base // unit + i for base, size in late for i in range(size // unit)]
    scale = jnp.sqrt(squares / model_width + norm_eps)
    rewards = along / scale
    picked = picked_rewards(rewards, partner)
    push = loss_scale * jax.nn.sigmoid(side * (rewards - picked))
    own_grad = side * push
    p1 = own_grad / scale
    p2 = own_grad * along / (model_width * scale * scale * scale)

    grad_gate, dy, g_state = call(
        functools.partial(gate_back_kernel, heads, hg, (len(late), len(blocks))),
        (groups,),
        [
            pl.BlockSpec((rows + 16, gw), lambda g: (0, g)),
            *[pl.BlockSpec((rows + 16, size), lambda g: (0, 0)) for _, size in late],
            *[pl.BlockSpec((unit, gw), lambda g, at=at: (at, g)) for at in blocks],
            segc_spec,
            segc_spec,
            cols,
            cols,
            row1,
            c_spec,
            packed_spec,
            row1,
        ],
        [cols, cols, pl.BlockSpec((STATE + 16, gw), lambda g: (0, g))],
        [
            shape((rows, channels), bf16),
            shape((rows, channels), bf16),
            shape((STATE + 16, channels), bf16),
        ],
        flops=2 * rows * STATE * channels,
        size=14 * rows * channels,
        limit=STREAM_LIMIT,
    )(
        dm,
        *hidden,
        *[out_weight] * len(blocks),
        p1,
        p2,
        y,
        gate_input,
        gain,
        maps,
        packed,
        th,
    )

    def beside_back(token):
        dxd, dc, dbp, t1 = call(
            functools.partial(within_back_kernel, heads),
            (groups,),
            [
                cols,
                b_spec,
                c_spec,
                packed_spec,
                per_gt,
                segc_spec,
                segr_spec,
                cols,
                state,
            ],
            [cols, b_spec, b_spec, token_spec()],
            [
                shape((rows, channels), f32),
                shape((rows, groups * STATE), bf16),
                shape((rows, groups * STATE), f32),
                shape(TOKEN, f32),
            ],
            after=(token,),
            flops=4 * rows * rows * channels,
            size=10 * rows * channels,
        )(ssd_input, maps, maps, packed, atg, segc, segr, dy, s_in)
        return (dxd, dc, dbp), (t1,)

    own_d, other_d, other_g, (dxd, dc, dbp) = chain(g_state, False, beside_back)

    grad_input, db, grad_dt, d_cum = call(
        functools.partial(final_kernel, heads, hg),
        (groups,),
        [
            smem(),
            half_spec,
            half_spec,
            pl.BlockSpec((STATE + 16, gw), lambda g: (0, g)),
            state,
            state,
            row1,
            cols,
            b_spec,
            cols,
            cols,
            cols,
            b_spec,
            packed_spec,
            row1,
        ],
        [cols, b_spec, per_g, per_g],
        [
            shape((rows, channels), bf16),
            shape((rows, groups * STATE), bf16),
            grp,
            grp,
        ],
        flops=4 * rows * STATE * channels,
        size=16 * rows * channels,
    )(
        place,
        own_d,
        other_d,
        other_g,
        s_in,
        s_msg,
        th,
        ssd_input,
        maps,
        dy,
        y,
        dxd,
        dbp,
        packed,
        skip,
    )
    grad_step = call(
        functools.partial(step_kernel, groups),
        (),
        [vmem()] * 5,
        vmem(),
        shape((rows, heads), f32),
    )(step_raw, bias2, decay2, grad_dt, d_cum)
    grad_maps = jnp.stack([db, dc], axis=1)
    return (rewards.reshape(rows), grad_input, grad_gate, grad_maps, grad_step)


def solution(mesh):
    return jax.shard_map(
        on_device,
        mesh=mesh,
        in_specs=(
            P("seq", "tensor"),
            P("seq", "tensor"),
            P("seq", None, "tensor"),
            P("seq", "tensor"),
            P("tensor"),
            P("tensor"),
            P("tensor"),
            P("tensor"),
            P(None, "tensor"),
            P(),
            P(),
            P(),
        ),
        out_specs=(
            P("seq"),
            P("seq", "tensor"),
            P("seq", "tensor"),
            P("seq", None, "tensor"),
            P("seq", "tensor"),
        ),
        check_vma=False,
    )
```

```python
import functools

import jax
import jax.numpy as jnp
from jax import lax
from jax.experimental import pallas as pl
from jax.experimental.pallas import tpu as pltpu
from jax.sharding import PartitionSpec as P

STATE = 128
BLK = 128
norm_eps = 1e-05
loss_scale = 64.0
f32 = jnp.float32
bf16 = jnp.bfloat16
VMEM_LIMIT = 24 * 1024 * 1024
STREAM_LIMIT = 49 * 1024 * 1024


def dot(a, b, ca, cb, precision=None):
    return lax.dot_general(
        a, b, (((ca,), (cb,)), ((), ())), precision=precision, preferred_element_type=f32
    )


MSG = f32


def dot_hi_lo(a, b, ca, cb):
    hi = a.astype(bf16)
    lo = (a - hi.astype(f32)).astype(bf16)
    return dot(hi, b, ca, cb) + dot(lo, b, ca, cb)


def rounded(v):
    return lax.reduce_precision(v, exponent_bits=8, mantissa_bits=7)


def split3(v):
    hi = rounded(v)
    mid = rounded(v - hi)
    lo = rounded(v - hi - mid)
    return hi, mid, lo


def split3_in(v):
    hi = v.astype(bf16).astype(f32)
    mid = (v - hi).astype(bf16).astype(f32)
    lo = (v - hi - mid).astype(bf16).astype(f32)
    return hi, mid, lo


def lanes(cols, width):
    rows = cols.shape[0]
    return jnp.concatenate(
        [jnp.broadcast_to(cols[:, h : h + 1], (rows, width)) for h in range(cols.shape[1])], axis=1
    )


def states_kernel(
    groups, off, lens, raw, bias, decay, x, maps, packed, atg, dttg, segc, segr, s_msg
):
    rows, heads = raw.shape
    hg = heads // groups
    width = x.shape[1] // heads
    v = raw[...] + bias[...]
    dt = jnp.maximum(v, 0.0) + jnp.log1p(jnp.exp(-jnp.abs(v)))
    e = -dt * decay[...]
    r = lax.broadcasted_iota(jnp.int32, (rows, rows), 0)
    c = lax.broadcasted_iota(jnp.int32, (rows, rows), 1)
    tril = (c <= r).astype(f32)
    cum = dot(tril, e, 1, 0, lax.Precision.HIGHEST)
    cum_t = dot(e, tril, 0, 1, lax.Precision.HIGHEST)
    eye = (c == r).astype(f32)
    dt_t = dot(dt, eye, 0, 0, lax.Precision.HIGHEST)
    pos = off[0] + lax.broadcasted_iota(jnp.int32, (rows, 128), 0)
    opening = jnp.int32(0)
    starts = jnp.zeros((rows, 128), f32)
    for k in range(lens.shape[0]):
        starts = jnp.where(pos == opening, 1.0, starts)
        opening = opening + lens[k]
    seg = dot(tril, starts, 1, 0)[:, :1]
    segc[...] = seg
    segr[...] = dot(starts, tril, 0, 1)[:8]
    seg_last = seg[rows - 1 : rows]
    last = cum[rows - 1 : rows]
    w = jnp.where(seg == seg_last, jnp.exp(last - cum), 0.0)
    f = jnp.where(seg == 0.0, jnp.exp(cum), 0.0)
    th = jnp.where(seg_last == 0.0, jnp.exp(last), 0.0)
    wdt = w * dt
    fill = jnp.zeros((rows, 128 - 4 * heads), f32)
    packed[...] = jnp.concatenate([dt, cum, f, w, fill], axis=1)
    for g in range(groups):
        hs = slice(g * hg, (g + 1) * hg)
        ls = slice(g * hg * width, (g + 1) * hg * width)
        atg[g] = cum_t[hs]
        dttg[g] = dt_t[hs]
        wx = lanes(wdt[:, hs], width) * x[:, ls].astype(f32)
        b_rows = maps[:, g * STATE : (g + 1) * STATE]
        wx_hi = wx.astype(bf16)
        wx_lo = (wx - wx_hi.astype(f32)).astype(bf16)
        s_msg[0:STATE, ls] = (dot(b_rows, wx_hi, 0, 0) + dot(b_rows, wx_lo, 0, 0)).astype(s_msg.dtype)
        if s_msg.dtype == f32:
            s_msg[STATE : STATE + 8, ls] = jnp.broadcast_to(
                lanes(th[:, hs], width), (8, hg * width)
            )
            continue
        hi, mid, lo = split3_in(lanes(th[:, hs], width))
        row = lax.broadcasted_iota(jnp.int32, (16, hg * width), 0)
        tail = jnp.where(row == 0, hi, jnp.where(row == 1, mid, jnp.where(row == 2, lo, 0.0)))
        s_msg[STATE : STATE + 16, ls] = tail.astype(bf16)


def head_columns(packed, heads, count):
    shift = (128 - count * pl.program_id(0)) % 128
    turned = pltpu.roll(packed[...], shift, 1)
    return [turned[:, k * heads : k * heads + count] for k in range(4)]


def mask_terms(segc, segr, i):
    size = (i + 1) * BLK
    r = i * BLK + lax.broadcasted_iota(jnp.int32, (BLK, size), 0)
    c = lax.broadcasted_iota(jnp.int32, (BLK, size), 1)
    ok = (c <= r) & (segc[i * BLK : (i + 1) * BLK, :] == segr[0:1, :size])
    return jnp.where(ok, 0.0, -1e30)


def within_kernel(heads, x, b, c, dtt, packed, atg, segc, segr, yw, token):
    token[...] = jnp.zeros_like(token)
    rows = x.shape[0]
    hg = atg.shape[1]
    _, cum, _, _ = head_columns(packed, heads, hg)
    width = x.shape[1] // hg
    for i in range(rows // BLK):
        ti, size = slice(i * BLK, (i + 1) * BLK), (i + 1) * BLK
        scores = dot(c[ti, :], b[:size, :], 1, 1)
        neg = mask_terms(segc, segr, i)
        for h in range(hg):
            decays = jnp.exp(cum[ti, h : h + 1] - atg[0, h : h + 1, :size] + neg)
            m = decays * scores * dtt[0, h : h + 1, :size]
            yw[ti, h * width : (h + 1) * width] = dot_hi_lo(
                m, x[:size, h * width : (h + 1) * width], 1, 0
            )


def sum3(rows):
    rows = rows.astype(f32)
    return (rows[0:1] + rows[1:2]) + rows[2:3]


def through_of(rows):
    if rows.dtype == f32:
        return rows[0:1]
    return sum3(rows)


def tail_of(through, kind):
    if kind == f32:
        return jnp.broadcast_to(through, (8, through.shape[1]))
    hi, mid, lo = split3_in(through)
    row = lax.broadcasted_iota(jnp.int32, (16, through.shape[1]), 0)
    tail = jnp.where(row == 0, hi, jnp.where(row == 1, mid, jnp.where(row == 2, lo, 0.0)))
    return tail.astype(bf16)


def pair_kernel(forward, place, message, other, out, far, token):
    core = place[0] % 2
    half = STATE // 2
    late = core if forward else 1 - core
    start = pl.multiple_of(core * half, half)
    mine, theirs = message[pl.ds(start, half), :], other[pl.ds(start, half), :]
    mine, theirs = mine.astype(f32), theirs.astype(f32)
    th_mine, th_theirs = through_of(message[STATE:, :]), through_of(other[STATE:, :])
    is_late = late == 1
    pair = jnp.where(is_late, mine + th_mine * theirs, theirs + th_theirs * mine)
    out[0:half, :] = pair.astype(out.dtype)
    out[half:, :] = tail_of(th_mine * th_theirs, out.dtype)
    far[...] = pair.astype(bf16)
    token[...] = jnp.zeros_like(token)


def enter_kernel(near, far, out):
    half = STATE // 2
    out[...] = (
        near[0:half, :].astype(f32) + through_of(near[half:, :]) * far[...].astype(f32)
    ).astype(out.dtype)


def arriving(core, late, own, other, msg):
    half = STATE // 2
    mine, theirs = own[...].astype(f32), other[...].astype(f32)
    low = jnp.where(core == 0, mine, theirs)
    high = jnp.where(core == 0, theirs, mine)
    whole = jnp.concatenate([low, high], axis=0)
    passed = msg[0:STATE, :].astype(f32) + through_of(msg[STATE:, :]) * whole
    return jnp.where(late == 1, passed, whole)


def gate_kernel(
    heads, hg, place, yw, x, z, c, packed, own, other, msg, skip, gain, y, mixed, s_in
):
    width = x.shape[1] // hg
    _, _, f, _ = head_columns(packed, heads, hg)
    state = arriving(place[0] % 2, place[0] % 2, own, other, msg)
    s_hi = state.astype(bf16)
    s_lo = (state - s_hi.astype(f32)).astype(bf16)
    s_in[...] = s_hi
    out = (
        yw[...]
        + lanes(f, width) * (dot(c[...], s_hi, 1, 0) + dot(c[...], s_lo, 1, 0))
        + skip[...] * x[...].astype(f32)
    )
    y[...] = out
    zf = z[...].astype(f32)
    gated = out * zf / (1.0 + jnp.exp(-zf))
    mean = jnp.mean(gated * gated, axis=1, keepdims=True)
    mixed[...] = (gated * lax.rsqrt(mean + norm_eps) * gain[...]).astype(bf16)


def add_products(value, hiddens, weights):
    at = 0
    for h in hiddens:
        for start in range(0, h.shape[1], weights[0].shape[0]):
            term = dot(h[:, start : start + weights[0].shape[0]], weights[at][...], 1, 0)
            value = term if value is None else value + term
            at += 1
    return value


def gate_back_kernel(
    heads, hg, count, dm, *refs
):
    hiddens, weights = refs[: count[0]], refs[count[0] : sum(count)]
    p1, p2, y, z, gain, c, packed, th, grad_z, dy, g_state = refs[sum(count) :]
    rows = z.shape[0]
    width = z.shape[1] // hg
    _, _, f, _ = head_columns(packed, heads, hg)
    products = add_products(dm[...], hiddens, weights)
    d_mixed = p1[...] * sum3(products[rows:]) - p2[...] * products[:rows]
    zf = z[...].astype(f32)
    sig = 1.0 / (1.0 + jnp.exp(-zf))
    silu = zf * sig
    yv = y[...]
    gated = yv * silu
    inv = lax.rsqrt(jnp.mean(gated * gated, axis=1, keepdims=True) + norm_eps)
    dn = d_mixed * gain[...]
    corr = jnp.mean(dn * gated, axis=1, keepdims=True)
    dgated = inv * dn - gated * (inv * inv * inv * corr)
    grad_z[...] = (dgated * yv * (sig * (1.0 + zf * (1.0 - sig)))).astype(bf16)
    dyv = (dgated * silu).astype(bf16)
    dy[...] = dyv
    fdy = (lanes(f, width) * dyv.astype(f32)).astype(bf16)
    g_state[0:STATE, :] = dot(c[...], fdy, 0, 0).astype(bf16)
    g_state[STATE:, :] = tail_of(th[...], bf16)


def within_back_kernel(
    heads, x, b, c, packed, atg, segc, segr, dy, s_in, dxd, dc, db, token
):
    rows = x.shape[0]
    hg = atg.shape[1]
    width = x.shape[1] // hg
    dt, cum, f, _ = head_columns(packed, heads, hg)
    xd = (lanes(dt, width) * x[...].astype(f32)).astype(bf16)
    dyv = dy[...]
    fdy = (lanes(f, width) * dyv.astype(f32)).astype(bf16)
    token[...] = jnp.zeros_like(token)
    carried = dot(fdy, s_in[...], 1, 1)
    for i in range(rows // BLK):
        ti, size = slice(i * BLK, (i + 1) * BLK), (i + 1) * BLK
        scores = dot(c[ti, :], b[:size, :], 1, 1)
        neg = mask_terms(segc, segr, i)
        total = jnp.zeros((BLK, size), f32)
        for h in range(hg):
            ls = slice(h * width, (h + 1) * width)
            decays = jnp.exp(cum[ti, h : h + 1] - atg[0, h : h + 1, :size] + neg)
            m = (decays * scores).astype(bf16)
            total = total + decays * dot(dyv[ti, ls], xd[:size, ls], 1, 1)
            back = dot(m, dyv[ti, ls], 0, 0)
            if i > 0:
                dxd[: i * BLK, ls] += back[: i * BLK]
            dxd[ti, ls] = back[i * BLK :]
        dgv = total.astype(bf16)
        dc[ti, :] = (carried[ti] + dot(dgv, b[:size, :], 1, 0)).astype(bf16)
        back = dot(dgv, c[ti, :], 0, 0)
        if i > 0:
            db[: i * BLK, :] += back[: i * BLK]
        db[ti, :] = back[i * BLK :]


def final_kernel(
    heads, hg, place, own, other, msg, s_in, s_loc, th, x, b, dy, y, dxd, dbp, packed, skip,
    grad_x, db, grad_dt, d_cum,
):
    rows = x.shape[0]
    width = x.shape[1] // hg
    dt, _, _, w = head_columns(packed, heads, hg)
    xf = x[...].astype(f32)
    dyv = dy[...].astype(f32)
    dtl = lanes(dt, width)
    wl = lanes(w, width)
    core = place[0] % 2
    dsv = arriving(core, 1 - core, own, other, msg).astype(bf16)
    bds = dot(b[...], dsv, 1, 0)
    wx = (wl * dtl * xf).astype(bf16)
    db[...] = (dbp[...] + dot(wx, dsv, 1, 1)).astype(bf16)
    q = dxd[...] + wl * bds
    grad_x[...] = (dtl * q + skip[...] * dyv).astype(bf16)
    xd = (dtl * xf).astype(bf16).astype(f32)
    direct = xf * q
    cums = dyv * (y[...] - skip[...] * xf) - xd * dxd[...] - wx.astype(f32) * bds
    ends = dsv.astype(f32) * (
        th[...] * s_in[...].astype(f32) + s_loc[...].astype(f32)
    )
    last = lax.broadcasted_iota(jnp.int32, (rows, 1), 0) == rows - 1
    for h in range(hg):
        ls = slice(h * width, (h + 1) * width)
        grad_dt[0, :, h : h + 1] = jnp.sum(direct[:, ls], axis=1, keepdims=True)
        end = jnp.sum(jnp.sum(ends[:, ls], axis=0, keepdims=True), axis=1, keepdims=True)
        d_cum[0, :, h : h + 1] = jnp.sum(cums[:, ls], axis=1, keepdims=True) + jnp.where(
            last, end, 0.0
        )


def step_kernel(groups, raw, bias, decay, grad_dt, d_cum, out):
    rows, heads = raw.shape
    r = lax.broadcasted_iota(jnp.int32, (rows, rows), 0)
    c = lax.broadcasted_iota(jnp.int32, (rows, rows), 1)
    triu = (c >= r).astype(f32)
    direct = jnp.concatenate([grad_dt[g] for g in range(groups)], axis=1)
    dcv = jnp.concatenate([d_cum[g] for g in range(groups)], axis=1)
    de = dot(triu, dcv, 1, 0, lax.Precision.HIGHEST)
    v = raw[...] + bias[...]
    out[...] = (direct - decay[...] * de) / (1.0 + jnp.exp(-v))


def as_row(column):
    return jnp.transpose(jnp.broadcast_to(column, (column.shape[0], 128)))[0:1]


def as_column(row):
    return jnp.transpose(jnp.broadcast_to(row, (128, row.shape[1])))[:, 0:1]


def row_tail(row, width):
    row = jnp.concatenate([row, jnp.zeros((1, width - row.shape[1]), f32)], axis=1)
    return tail_of(row, bf16)


def project_kernel(mixed, w, head, before, out, along, token):
    rows = mixed.shape[0]
    value = dot(mixed[...], w[...], 1, 1)
    out[:rows, :] = value.astype(bf16)
    part = jnp.sum(value * head[...], axis=1, keepdims=True)
    along[...] = part + jnp.where(pl.program_id(0) == 0, before[...], along[...])
    if out.shape[0] > rows:
        out[rows:, :] = row_tail(as_row(along[...]), out.shape[1])
    token[...] = jnp.zeros_like(token)


def add_kernel(rows, a, b, out, token):
    out[:rows, :] = (a[:rows, :].astype(f32) + b[:rows, :].astype(f32)).astype(bf16)
    if rows < a.shape[0]:
        out[rows:, :] = tail_of(sum3(a[rows:, :]) + sum3(b[rows:, :]), bf16)
    token[...] = jnp.zeros_like(token)


def choose_kernel(rows, place, total, got, heads3, before, hidden, squares, token, *along):
    middle = (place[0] == 1) | (place[0] == 2)
    h = jnp.where(middle, total[:rows, :].astype(f32), got[:rows, :].astype(f32))
    if along:
        row = jnp.where(middle, sum3(total[rows:, :]), sum3(got[rows:, :]))
        along[0][...] = as_column(row[:, :rows])
    hidden[:rows, :] = h.astype(bf16)
    hidden[rows:, :] = heads3[...]
    squares[...] = before[...] + jnp.sum(h * h, axis=1, keepdims=True)
    token[...] = jnp.zeros_like(token)


def back_kernel(count, first, *refs):
    hiddens, weights, refs = refs[: count[0]], refs[count[0] : sum(count)], refs[sum(count) :]
    before, out, token = (None,) + refs if first else refs
    token[...] = jnp.zeros_like(token)
    out[...] = add_products(None if first else before[...], hiddens, weights)


def partner_kernel(off, pairs, out):
    rows, total = out.shape[0], pairs.shape[1]
    v = jnp.broadcast_to(pairs[...].astype(f32), (8, total))
    even = lax.broadcasted_iota(jnp.int32, (8, total), 1) % 2 == 0
    signed = jnp.where(even, -1.0 - pltpu.roll(v, total - 1, 1), 1.0 + pltpu.roll(v, 1, 1))
    tokens = (off[0] + lax.broadcasted_iota(jnp.int32, (rows, 1), 0)).astype(f32)
    acc = jnp.zeros((rows, 128), f32)
    for k in range(total // 128):
        ls = slice(k * 128, (k + 1) * 128)
        acc = acc + jnp.where(tokens == v[0:1, ls], signed[0:1, ls], 0.0)
    out[...] = jnp.sum(acc, axis=1, keepdims=True)


def vmem():
    return pl.BlockSpec(memory_space=pltpu.VMEM)


def smem():
    return pl.BlockSpec(memory_space=pltpu.SMEM)


def token_spec():
    return pl.BlockSpec((8, 128), lambda *at: (0, 0))


def call(
    kernel, grid, ins, outs, shapes, after=(), aliases=None, flops=0, size=0, limit=VMEM_LIMIT
):
    count = len(after)
    inner = (lambda *refs: kernel(*refs[count:])) if count else kernel
    run = pl.pallas_call(
        inner,
        grid=grid,
        in_specs=[pl.BlockSpec(memory_space=pl.ANY)] * count + list(ins),
        out_specs=outs,
        out_shape=shapes,
        input_output_aliases={k + count: v for k, v in (aliases or {}).items()},
        compiler_params=pltpu.CompilerParams(vmem_limit_bytes=limit),
        cost_estimate=pl.CostEstimate(flops=flops // 4, bytes_accessed=size // 4, transcendentals=0),
    )
    return lambda *args: run(*after, *args)


def shape(dims, kind):
    return jax.ShapeDtypeStruct(dims, kind)


TOKEN = (8, 128)


def hops(count, distance):
    return [(i, i + distance) for i in range(count) if 0 <= i + distance < count]


def chain(message, forward, beside):
    count, place = lax.axis_size("seq"), lax.axis_index("seq").reshape(1)
    kind = message.dtype
    half = STATE // 2
    swap = [(i, i ^ 1) for i in range(count)]
    other = lax.ppermute(message, "seq", swap)
    pair_rows = half + message.shape[0] - STATE
    pair, pair_far, token = call(
        functools.partial(pair_kernel, forward),
        (),
        [smem(), vmem(), vmem()],
        [vmem(), vmem(), vmem()],
        [
            shape((pair_rows, message.shape[1]), kind),
            shape((half, message.shape[1]), bf16),
            shape(TOKEN, f32),
        ],
    )(place, message, other)
    way = 1 if forward else -1
    near = lax.ppermute(pair, "seq", hops(count, 2 * way))
    far = lax.ppermute(pair_far, "seq", hops(count, 4 * way))
    results, tokens = beside(token)
    own = call(
        enter_kernel,
        (),
        [vmem(), vmem()],
        vmem(),
        shape((half, message.shape[1]), kind),
        after=tokens,
    )(near, far)
    return own, lax.ppermute(own, "seq", swap), other, results


def pieces(count):
    unit = count // 8
    return [(unit * at, unit * size) for at, size in ((0, 1), (1, 2), (3, 2), (5, 2), (7, 1))]


def hidden_products(mixed, out_weight, reward_head):
    count, place = lax.axis_size("tensor"), lax.axis_index("tensor").reshape(1)
    rows, channels = mixed.shape
    model_width = out_weight.shape[0]
    plan = pieces(model_width)
    unit = model_width // 8
    line = count == 4
    tile = min(512, channels)
    column, column_spec = shape((rows, 1), f32), pl.BlockSpec((rows, 1), lambda j: (0, 0))
    head = reward_head[None, :]
    heads3 = jnp.concatenate(
        list(split3(head)) + [jnp.zeros((13, model_width), f32)], axis=0
    ).astype(bf16)

    def project(base, size, before, after, tail):
        step = size if tail else size // 2
        return call(
            project_kernel,
            (size // step,),
            [
                pl.BlockSpec((rows, channels), lambda j: (0, 0)),
                pl.BlockSpec((step, channels), lambda j: (base // step + j, 0)),
                pl.BlockSpec((1, step), lambda j: (0, base // step + j)),
                column_spec,
            ],
            [
                pl.BlockSpec((rows + 16 * tail, step), lambda j: (0, j)),
                column_spec,
                token_spec(),
            ],
            [shape((rows + 16 * tail, size), bf16), column, shape(TOKEN, f32)],
            after=after,
            flops=2 * rows * channels * size,
            size=2 * channels * size,
            limit=STREAM_LIMIT,
        )(mixed, out_weight, head, before)

    def add(a, b, after):
        return call(
            functools.partial(add_kernel, rows),
            (),
            [vmem(), vmem()],
            [vmem(), vmem()],
            [shape(a.shape, bf16), shape(TOKEN, f32)],
            after=after,
            size=6 * a.size,
        )(a, b)

    def choose(k, total, got, squares, after):
        base, size = plan[k]
        tail = total.shape[0] > rows
        return call(
            functools.partial(choose_kernel, rows),
            (),
            [smem()] + [vmem()] * 4,
            [vmem()] * (3 + tail),
            [shape((rows + 16, size), bf16), column, shape(TOKEN, f32)] + [column] * tail,
            after=after,
            size=6 * total.size,
        )(place, total, got, heads3[:, base : base + size], squares)

    def back(hiddens, parts, before, after):
        first = before is None
        wide = pl.BlockSpec((rows + 16, tile), lambda j: (0, j))
        ins = [pl.BlockSpec((rows + 16, size), lambda j: (0, 0)) for _, size in parts]
        blocks = [base // unit + i for base, size in parts for i in range(size // unit)]
        ins += [pl.BlockSpec((unit, tile), lambda j, at=at: (at, j)) for at in blocks]
        total = unit * len(blocks)
        return call(
            functools.partial(back_kernel, (len(parts), len(blocks)), first),
            (channels // tile,),
            ins if first else ins + [wide],
            [wide, token_spec()],
            [shape((rows + 16, channels), f32), shape(TOKEN, f32)],
            after=after,
            aliases=None if first else {len(ins): 0},
            flops=2 * rows * channels * total,
            size=2 * channels * total + 8 * rows * channels,
            limit=STREAM_LIMIT,
        )(*hiddens, *[out_weight] * len(blocks), *(() if first else (before,)))

    squares = jnp.zeros((rows, 1), f32)
    along = jnp.zeros((rows, 1), f32)
    last = len(plan) - 1
    held = []
    if not line:
        for k, (base, size) in enumerate(plan):
            part, along, _ = project(base, size, along, (), False)
            h = lax.psum(part.astype(f32), "tensor").astype(bf16)
            squares = squares + jnp.sum(jnp.square(h.astype(f32)), axis=1, keepdims=True)
            h = jnp.concatenate([h, heads3[:, base : base + size]], axis=0)
            held.append(h)
        dm, _ = back(held[:-2], plan[:-2], None, ())
        return dm, held[-2:], squares, lax.psum(along, "tensor")
    outward, across, inward = [(1, 0), (2, 3)], [(1, 2), (2, 1)], [(0, 1), (3, 2)]
    own, moved, sums, crossed, totals, got = {}, {}, {}, {}, {}, {}
    after = ()

    def start(k, along, after):
        own[k], along, token = project(*plan[k], along, after, k == last)
        moved[k] = lax.ppermute(own[k], "tensor", inward)
        return along, (token,)

    ahead = 2
    for k in range(ahead):
        along, after = start(k, along, after)
    for slot in range(len(plan) + 2):
        k = slot
        if k <= last:
            sums[k], token = add(own[k], moved[k], after)
            crossed[k] = lax.ppermute(sums[k], "tensor", across)
            after = (token,)
        if slot + ahead <= last:
            along, after = start(slot + ahead, along, after)
        k = slot - 1
        if 0 <= k <= last:
            totals[k], token = add(sums[k], crossed[k], after)
            got[k] = lax.ppermute(totals[k], "tensor", outward)
            after = (token,)
        if slot == last + 1:
            dm, token = back(held, plan[: len(held)], None, after)
            after = (token,)
        k = slot - 2
        if 0 <= k <= last:
            h, squares, token, *column_out = choose(k, totals[k], got[k], squares, after)
            held.append(h)
            after = (token,)

    return dm, held[-2:], squares, column_out[0]


def picked_rewards(rewards, partner):
    rows = rewards.shape[0]
    count, place = lax.axis_size("seq"), lax.axis_index("seq")
    flat = rewards.reshape(rows)
    other = lax.ppermute(flat, "seq", [(i, i ^ 1) for i in range(count)])
    even = place % 2 == 0
    both = jnp.concatenate([jnp.where(even, flat, other), jnp.where(even, other, flat)])
    total = jnp.zeros((rows, 1), f32)
    for d in range(count // 2):
        seen = both
        if d:
            seen = lax.ppermute(both, "seq", [(i, i ^ (2 * d)) for i in range(count)])
        base = ((place // 2) ^ d) * 2 * rows
        at = (base + jnp.arange(2 * rows, dtype=jnp.int32)).astype(f32)
        total = total + jnp.sum(
            jnp.where(partner == at[None, :], seen[None, :], 0.0), axis=1, keepdims=True
        )
    return total


def on_device(
    ssd_input,
    gate_input,
    state_maps,
    step_raw,
    step_bias,
    decay_rate,
    skip_gain,
    norm_gain,
    out_weight,
    reward_head,
    traj_lengths,
    step_pairs,
):
    rows, channels = ssd_input.shape
    heads = step_raw.shape[1]
    width = channels // heads
    groups = state_maps.shape[2] // STATE
    hg = heads // groups
    gw = hg * width
    model_width = out_weight.shape[0]
    offset = lax.axis_index("seq") * rows
    maps = state_maps.reshape(rows, 2 * groups * STATE)
    bias2, decay2 = step_bias[None, :], decay_rate[None, :]
    skip = jnp.repeat(skip_gain, width)[None, :]
    gain = norm_gain[None, :]

    cols = pl.BlockSpec((rows, gw), lambda g: (0, g))
    row1 = pl.BlockSpec((1, gw), lambda g: (0, g))
    b_spec = pl.BlockSpec((rows, STATE), lambda g: (0, g))
    c_spec = pl.BlockSpec((rows, STATE), lambda g: (0, groups + g))
    state = pl.BlockSpec((STATE, gw), lambda g: (0, g))
    per_g = pl.BlockSpec((1, rows, hg), lambda g: (g, 0, 0))
    packed_spec = pl.BlockSpec((rows, 128), lambda g: (0, 0))
    per_gt = pl.BlockSpec((1, hg, rows), lambda g: (g, 0, 0))
    segc_spec = pl.BlockSpec((rows, 1), lambda g: (0, 0))
    segr_spec = pl.BlockSpec((8, rows), lambda g: (0, 0))
    grp = shape((groups, rows, hg), f32)

    packed, atg, dttg, segc, segr, s_msg = call(
        functools.partial(states_kernel, groups),
        (),
        [smem(), smem(), vmem(), vmem(), vmem(), vmem(), vmem()],
        [vmem()] * 6,
        [
            shape((rows, 128), f32),
            shape((groups, hg, rows), f32),
            shape((groups, hg, rows), f32),
            shape((rows, 1), f32),
            shape((8, rows), f32),
            shape((STATE + 16 if MSG == bf16 else STATE + 8, channels), MSG),
        ],
    )(offset.reshape(1), traj_lengths, step_raw, bias2, decay2, ssd_input, maps)

    place = lax.axis_index("seq").reshape(1)
    th = s_msg[STATE : STATE + 1]
    total = step_pairs.shape[0]

    def beside_forward(token):
        yw, t1 = call(
            functools.partial(within_kernel, heads),
            (groups,),
            [cols, b_spec, c_spec, per_gt, packed_spec, per_gt, segc_spec, segr_spec],
            [cols, token_spec()],
            [shape((rows, channels), f32), shape(TOKEN, f32)],
            after=(token,),
            flops=2 * rows * rows * channels,
            size=8 * rows * channels,
        )(ssd_input, maps, maps, dttg, packed, atg, segc, segr)
        found = call(
            partner_kernel,
            (),
            [smem(), vmem()],
            vmem(),
            shape((rows, 1), f32),
            after=(t1,),
        )(offset.reshape(1), step_pairs.reshape(1, total))
        return (yw, found), (found,)

    own_s, other_s, other_msg, (yw, found) = chain(s_msg, True, beside_forward)
    partner = jnp.abs(found) - 1.0
    side = jnp.where(found < 0, -1.0, 1.0)

    tail = s_msg.shape[0]
    half_spec = pl.BlockSpec((STATE // 2, gw), lambda g: (0, g))
    y, mixed, s_in = call(
        functools.partial(gate_kernel, heads, hg),
        (groups,),
        [
            smem(),
            cols,
            cols,
            cols,
            c_spec,
            packed_spec,
            half_spec,
            half_spec,
            pl.BlockSpec((tail, gw), lambda g: (0, g)),
            row1,
            row1,
        ],
        [cols, cols, state],
        [
            shape((rows, channels), f32),
            shape((rows, channels), bf16),
            shape((STATE, channels), bf16),
        ],
        flops=2 * rows * STATE * channels,
        size=14 * rows * channels,
    )(
        place,
        yw,
        ssd_input,
        gate_input,
        maps,
        packed,
        own_s,
        other_s,
        other_msg,
        skip,
        gain,
    )

    dm, hidden, squares, along = hidden_products(
        mixed, out_weight, reward_head
    )
    unit = model_width // 8
    late = pieces(model_width)[-2:]
    blocks = [base // unit + i for base, size in late for i in range(size // unit)]
    scale = jnp.sqrt(squares / model_width + norm_eps)
    rewards = along / scale
    picked = picked_rewards(rewards, partner)
    push = loss_scale * jax.nn.sigmoid(side * (rewards - picked))
    own_grad = side * push
    p1 = own_grad / scale
    p2 = own_grad * along / (model_width * scale * scale * scale)

    grad_gate, dy, g_state = call(
        functools.partial(gate_back_kernel, heads, hg, (len(late), len(blocks))),
        (groups,),
        [
            pl.BlockSpec((rows + 16, gw), lambda g: (0, g)),
            *[pl.BlockSpec((rows + 16, size), lambda g: (0, 0)) for _, size in late],
            *[pl.BlockSpec((unit, gw), lambda g, at=at: (at, g)) for at in blocks],
            segc_spec,
            segc_spec,
            cols,
            cols,
            row1,
            c_spec,
            packed_spec,
            row1,
        ],
        [cols, cols, pl.BlockSpec((STATE + 16, gw), lambda g: (0, g))],
        [
            shape((rows, channels), bf16),
            shape((rows, channels), bf16),
            shape((STATE + 16, channels), bf16),
        ],
        flops=2 * rows * STATE * channels,
        size=14 * rows * channels,
        limit=STREAM_LIMIT,
    )(
        dm,
        *hidden,
        *[out_weight] * len(blocks),
        p1,
        p2,
        y,
        gate_input,
        gain,
        maps,
        packed,
        th,
    )

    def beside_back(token):
        dxd, dc, dbp, t1 = call(
            functools.partial(within_back_kernel, heads),
            (groups,),
            [
                cols,
                b_spec,
                c_spec,
                packed_spec,
                per_gt,
                segc_spec,
                segr_spec,
                cols,
                state,
            ],
            [cols, b_spec, b_spec, token_spec()],
            [
                shape((rows, channels), f32),
                shape((rows, groups * STATE), bf16),
                shape((rows, groups * STATE), f32),
                shape(TOKEN, f32),
            ],
            after=(token,),
            flops=4 * rows * rows * channels,
            size=10 * rows * channels,
        )(ssd_input, maps, maps, packed, atg, segc, segr, dy, s_in)
        return (dxd, dc, dbp), (t1,)

    own_d, other_d, other_g, (dxd, dc, dbp) = chain(g_state, False, beside_back)

    grad_input, db, grad_dt, d_cum = call(
        functools.partial(final_kernel, heads, hg),
        (groups,),
        [
            smem(),
            half_spec,
            half_spec,
            pl.BlockSpec((STATE + 16, gw), lambda g: (0, g)),
            state,
            state,
            row1,
            cols,
            b_spec,
            cols,
            cols,
            cols,
            b_spec,
            packed_spec,
            row1,
        ],
        [cols, b_spec, per_g, per_g],
        [
            shape((rows, channels), bf16),
            shape((rows, groups * STATE), bf16),
            grp,
            grp,
        ],
        flops=4 * rows * STATE * channels,
        size=16 * rows * channels,
    )(
        place,
        own_d,
        other_d,
        other_g,
        s_in,
        s_msg,
        th,
        ssd_input,
        maps,
        dy,
        y,
        dxd,
        dbp,
        packed,
        skip,
    )
    grad_step = call(
        functools.partial(step_kernel, groups),
        (),
        [vmem()] * 5,
        vmem(),
        shape((rows, heads), f32),
    )(step_raw, bias2, decay2, grad_dt, d_cum)
    grad_maps = jnp.stack([db, dc], axis=1)
    return (rewards.reshape(rows), grad_input, grad_gate, grad_maps, grad_step)


def solution(mesh):
    return jax.shard_map(
        on_device,
        mesh=mesh,
        in_specs=(
            P("seq", "tensor"),
            P("seq", "tensor"),
            P("seq", None, "tensor"),
            P("seq", "tensor"),
            P("tensor"),
            P("tensor"),
            P("tensor"),
            P("tensor"),
            P(None, "tensor"),
            P(),
            P(),
            P(),
        ),
        out_specs=(
            P("seq"),
            P("seq", "tensor"),
            P("seq", "tensor"),
            P("seq", None, "tensor"),
            P("seq", "tensor"),
        ),
        check_vma=False,
    )
```
